256 devices in a mesh: dp: 8 (over z_lo, core), tm: 32 (over x, y, z_hi).
Axes of the slice: x: 4, y: 4, z: 8 (z_hi: 2, z_lo: 4; z = z_hi * 4 + z_lo), core: 2. Of those that a mesh axis runs over, the one named last changes fastest.
Arguments:
- latents: bfloat16 [8, 128, 256, 512], P('dp', 'tm'), may hold values from -6 to 6
- upstream: bfloat16 [8, 128, 256, 512], P('dp', 'tm'), may hold values from -6 to 6
- conv_weight: bfloat16 [3, 512, 512], replicated, may hold values from -0.15625 to 0.15625
- w_query: bfloat16 [512, 512], replicated, may hold values from -20 to 20
- w_key: bfloat16 [512, 512], replicated, may hold values from -1 to 1
- w_value: bfloat16 [512, 512], replicated, may hold values from -0.25 to 0.25
- w_out: bfloat16 [512, 512], replicated, may hold values from -0.25 to 0.25
- norm_gain: float32 [512], replicated, may hold values from 0.1 to 1.9
Outputs:
- grad_latents: bfloat16 [8, 128, 256, 512], P('dp', 'tm')
- grad_conv: float32 [3, 512, 512], P(None, 'tm')
- grad_query: float32 [512, 512], P('tm')
- grad_key: float32 [512, 512], P('tm')
- grad_value: float32 [512, 512], P('tm')
- grad_out: float32 [512, 512], P('tm')
- grad_gain: float32 [512], P('tm')
The draws below stay inside these ranges and needn't reach their ends.
All inputs are finite; a program needn't handle non-finite values.
Results may differ from the reference program's by a relative error of at most 0.013.
Values may be sent and summed in bfloat16 or wider, within the bound.
A program may use at most 128 MiB of HBM per device.

```python
import jax
import jax.numpy as jnp
from jax import lax

C = 512
HEADS = 8
FRAMES = 128
PIXELS = 256
CLIPS = 8


def shared_matrix(key):
    return jnp.clip(jax.random.normal(key, (C, C), jnp.float32), -6.0, 6.0) * C ** (-0.5)


def draw_w_key(key, part):
    shared = shared_matrix(key)
    return shared.astype(jnp.bfloat16)


def draw_w_query(key, part):
    key = jax.random.fold_in(key, 7)
    first = jax.random.fold_in(key, 0)
    own = jnp.clip(jax.random.normal(first, (C, C), jnp.float32), -6.0, 6.0) * C ** (-0.5)
    return own.astype(jnp.bfloat16)


def strengthened(entries, key, source, target, shards_of, factor):
    owner, partner = [(jnp.arange(entries.shape[axis_at]) // (entries.shape[axis_at] // shards_of)).reshape([-1 if axis == axis_at else 1 for axis in range(entries.ndim)]) for axis_at in (source, target)]
    chosen = jax.random.permutation(key, shards_of)[partner]
    strong = (owner == chosen) | (owner == (partner + shards_of // 2) % shards_of)
    return jnp.where(strong, factor * entries, entries)


def levels(key, extent, cuts, low, largest):
    level, own = 1.0, jax.random.fold_in(key, 6)
    for dim, shards_of in cuts:
        heights = jnp.exp(jax.random.uniform(jax.random.fold_in(own, dim), (shards_of,), jnp.float32, low / len(cuts), largest / len(cuts)))
        level = level * jnp.repeat(heights, extent[dim] // shards_of).reshape([-1 if axis == dim else 1 for axis in range(len(extent))])
    return level


def bell_draw(own_key, extent, spread, bound, shards=(), held_as=jnp.bfloat16):
    factor_of = levels(own_key, extent, shards, -0.22, 0.18) if shards else 1.0
    result = jax.random.normal(own_key, extent, jnp.float32) * spread * factor_of
    return jnp.minimum(jnp.maximum(result, -bound), bound).astype(held_as)


def bell_draw_with(key, extent, deviation, bound, cuts, heavy, held_as=jnp.bfloat16):
    result = deviation * jax.random.normal(key, extent, jnp.float32)
    if cuts:
        result = result * levels(key, extent, cuts, -0.22, 0.18)
    return jnp.clip(strengthened(result, jax.random.fold_in(key, 3), *heavy), -bound, bound).astype(held_as)


def setup_inputs(seed: int = 0) -> dict:
    streams_of = jax.random.split(jax.random.key(seed), 9)
    return {
        "latents": bell_draw(streams_of[0], (CLIPS, FRAMES, PIXELS, C), 1.0, 6.0, ((0, 8), (1, 32))),
        "upstream": bell_draw_with(streams_of[1], (CLIPS, FRAMES, PIXELS, C), 1.0, 6.0, ((0, 8), (1, 32)), (1, 3, 32, 2.75)),
        "conv_weight": bell_draw(streams_of[2], (3, C, C), (3 * C) ** -0.5, 0.15625),
        "w_query": draw_w_query(jax.random.fold_in(streams_of[8], 71), 0),
        "w_key": draw_w_key(jax.random.fold_in(streams_of[8], 71), 0),
        "w_value": bell_draw(streams_of[5], (C, C), C ** -0.5, 0.25),
        "w_out": bell_draw(streams_of[6], (C, C), C ** -0.5, 0.25),
        "norm_gain": jnp.clip(1.0 + 0.18 * jax.random.normal(streams_of[7], (C,), jnp.float32), 0.1, 1.9),
    }


def cross(left, right):
    return lax.dot_general(left, right, (((0,), (0,)), ((), ())), preferred_element_type=jnp.float32)

def attend_back(mid, upstream_clip, w_query, w_key, w_value, w_out, norm_gain):
    nframes, npix, width = mid.shape
    shape4 = (nframes, npix, HEADS, width // HEADS)
    scale = (width // HEADS) ** (-0.5)
    upper = mid.reshape(-1, width).astype(jnp.float32)
    rinv = lax.rsqrt(lax.optimization_barrier(jnp.mean(upper * upper, -1, keepdims=True)) + 1e-06)
    normed = (upper * rinv * norm_gain).astype(jnp.bfloat16)
    query = jnp.dot(normed, w_query, preferred_element_type=jnp.float32).astype(jnp.bfloat16)
    keyed = jnp.dot(normed, w_key, preferred_element_type=jnp.float32).astype(jnp.bfloat16)
    valued = jnp.dot(normed, w_value, preferred_element_type=jnp.float32).astype(jnp.bfloat16)
    q4 = query.reshape(shape4).astype(jnp.float32)
    k4 = keyed.reshape(shape4).astype(jnp.float32)
    v4 = valued.reshape(shape4).astype(jnp.float32)
    scores = jnp.einsum('fphd,gphd->phfg', q4, k4) * scale
    probs = jax.nn.softmax(scores, -1)
    probs_b = probs.astype(jnp.bfloat16)
    attended = jnp.einsum('phfg,gphd->fphd', probs_b.astype(jnp.float32), v4).astype(jnp.bfloat16).reshape(-1, width)
    flat_up = upstream_clip.reshape(-1, width)
    grad_out = cross(attended, flat_up)
    d_att = jnp.dot(flat_up, w_out.T, preferred_element_type=jnp.float32).astype(jnp.bfloat16)
    da4 = d_att.reshape(shape4).astype(jnp.float32)
    d_probs = jnp.einsum('fphd,gphd->phfg', da4, v4)
    d_valued = jnp.einsum('phfg,fphd->gphd', probs_b.astype(jnp.float32), da4).astype(jnp.bfloat16)
    d_scores = (probs * (d_probs - lax.optimization_barrier(jnp.sum(probs * d_probs, -1, keepdims=True))) * scale).astype(jnp.bfloat16)
    ds32 = d_scores.astype(jnp.float32)
    d_query = jnp.einsum('phfg,gphd->fphd', ds32, k4).astype(jnp.bfloat16)
    d_keyed = jnp.einsum('phfg,fphd->gphd', ds32, q4).astype(jnp.bfloat16)
    joined = jnp.concatenate([d_query.reshape(-1, width), d_keyed.reshape(-1, width), d_valued.reshape(-1, width)], 1)
    weights = jnp.concatenate([w_query, w_key, w_value], 1)
    grads = cross(normed, joined)
    d_normed = jnp.dot(joined, weights.T, preferred_element_type=jnp.float32)
    gain_term = lax.optimization_barrier(jnp.sum(d_normed * upper * rinv, 0))
    scaled = norm_gain * d_normed
    d_mid = flat_up.astype(jnp.float32) + rinv * scaled - upper * rinv ** 3 * lax.optimization_barrier(jnp.mean(scaled * upper, -1, keepdims=True))
    d_mid = d_mid.astype(jnp.bfloat16).reshape(mid.shape)
    stacked = jnp.stack([grads[:, :width], grads[:, width:2 * width], grads[:, 2 * width:], grad_out])
    return (d_mid, stacked, gain_term)

def one_clip(latent_clip, upstream_clip, conv_weight, w_query, w_key, w_value, w_out, norm_gain):
    nframes, npix, width = latent_clip.shape
    padded = jnp.pad(latent_clip, ((1, 1), (0, 0), (0, 0)))
    conv = sum((jnp.dot(padded[k:k + nframes].reshape(-1, width), conv_weight[k], preferred_element_type=jnp.float32) for k in range(3)))
    mid = (latent_clip.reshape(-1, width).astype(jnp.float32) + conv).astype(jnp.bfloat16).reshape(latent_clip.shape)
    d_mid, stacked, gain_term = attend_back(mid, upstream_clip, w_query, w_key, w_value, w_out, norm_gain)
    grad_pad = jnp.pad(d_mid, ((1, 1), (0, 0), (0, 0)))
    back = sum((jnp.dot(grad_pad[2 - k:2 - k + nframes].reshape(-1, width), conv_weight[k].T, preferred_element_type=jnp.float32) for k in range(3)))
    grad_in = (d_mid.reshape(-1, width).astype(jnp.float32) + back).astype(jnp.bfloat16).reshape(latent_clip.shape)
    flat_mid = d_mid.reshape(-1, width)
    taps = jnp.stack([cross(padded[k:k + nframes].reshape(-1, width), flat_mid) for k in range(3)])
    return (grad_in, taps, stacked, gain_term)

def reference(latents, upstream, conv_weight, w_query, w_key, w_value, w_out, norm_gain):

    def step(pair):
        return one_clip(pair[0], pair[1], conv_weight, w_query, w_key, w_value, w_out, norm_gain)
    grad_in, taps, stacked, gain_term = lax.map(step, (latents, upstream))
    taps = lax.optimization_barrier(jnp.sum(taps, 0))
    stacked = lax.optimization_barrier(jnp.sum(stacked, 0))
    gain_term = lax.optimization_barrier(jnp.sum(gain_term, 0))
    return (grad_in, taps, stacked[0], stacked[1], stacked[2], stacked[3], gain_term)
```

```python
import jax
import jax.numpy as jnp
from jax import lax
from jax.experimental import pallas as pl
from jax.experimental.pallas import tpu as pltpu
from jax.sharding import PartitionSpec as P

C = 512
F = 128
TM = 32
BF = jnp.bfloat16
F32 = jnp.float32
MESH_ID = pl.DeviceIdType.MESH


def nn(a, b):
    return lax.dot_general(a, b, (((1,), (0,)), ((), ())), preferred_element_type=F32)


def nt(a, b):
    return lax.dot_general(a, b, (((1,), (1,)), ((), ())), preferred_element_type=F32)


def tn(a, b):
    return lax.dot_general(a, b, (((0,), (0,)), ((), ())), preferred_element_type=F32)


def where_am_i():
    dp, tm = lax.axis_index("dp"), lax.axis_index("tm")
    return dict(dp=dp, tm=tm, zl=dp // 2, c=dp % 2, x=tm // 8, y=(tm // 2) % 4, zh=tm % 2)


def device(zl, c, x, y, zh):
    return {"dp": zl * 2 + c, "tm": (x * 4 + y) * 2 + zh}


def signal(sem, dev):
    pl.semaphore_signal(sem, inc=1, device_id=dev, device_id_type=MESH_ID)


def send(src, dst, ssem, rsem, dev):
    pltpu.make_async_remote_copy(
        src_ref=src, dst_ref=dst, send_sem=ssem, recv_sem=rsem,
        device_id=dev, device_id_type=MESH_ID,
    ).start()


def wait_bytes(ref, sem):
    pltpu.make_async_copy(ref, ref, sem).wait()


def row_of(shape):
    return lax.broadcasted_iota(jnp.int32, shape, 0)


def split_heads(a):
    lane = lax.broadcasted_iota(jnp.int32, a.shape, 1)
    zero = jnp.zeros_like(a)
    return jnp.concatenate([jnp.where(lane < 64, a, zero), jnp.where(lane < 64, zero, a)], 0)


def join_heads(a):
    lane = lax.broadcasted_iota(jnp.int32, (F, 128), 1)
    return jnp.where(lane < 64, a[:F], a[F:])


def kernel(
    lat, up, wc, wq, wk, wv, wo, gain,
    out, ograds, ogain,
    sbl, sbu, rl, ru, osend, orecv,
    t32, x_s, mid_s, nrm_s, qkv_s, pr_s, att_s, up_s, da_s, dqkv_s, dm_s,
    g_s, gain_s, g0s_a, g0s_b, g0r_a, g0r_b,
    s1_a, r1_a, s2_a, r2_a, s1_b, r1_b, s2_b, r2_b,
    t_s, zr, zsum, agr, gn_s, gn0, gnx, gny, gnz,
    ssem, rsem,
):
    w = where_am_i()
    me, c, x, y, zl, zh = w["tm"], w["c"], w["x"], w["y"], w["zl"], w["zh"]
    z = zh * 4 + zl

    def at_z(zz, cc):
        return device(zz % 4, cc, x, y, zz // 4)

    barrier = pltpu.get_barrier_semaphore()

    @pl.loop(1, TM)
    def _(k):
        signal(barrier, {"dp": w["dp"], "tm": (me + k) % TM})

    signal(barrier, device(zl, 1 - c, x, y, zh))

    @pl.loop(1, 8)
    def _(k):
        @pl.when(k != 4)
        def _():
            signal(barrier, at_z((z + k) % 8, c))

    @pl.loop(1, 4)
    def _(k):
        signal(barrier, at_z(zh * 4 + (zl + k) % 4, 1 - c))

    def regroup(src, dst, h):
        a = [src[f, 128 * h:128 * h + 128, :].astype(F32) for f in range(4)]
        low = row_of((F, C)) % 8 < 4
        tiles = []
        for f in (0, 2):
            even = jnp.where(low, a[f], pltpu.roll(a[f + 1], 4, 0))
            odd = jnp.where(low, pltpu.roll(a[f], F - 4, 0), a[f + 1])
            tiles.append((even.reshape(16, 8, C), odd.reshape(16, 8, C)))
        for m in range(16):
            for o in range(2):
                dst[h, 2 * m + o] = jnp.concatenate(
                    [tiles[0][o][m], tiles[1][o][m]], 0
                ).astype(BF)

    def scatter(src, dst, h, i):
        @pl.loop(1, TM)
        def _(k):
            to = (me + k) % TM
            send(src.at[h, to], dst.at[h, me], ssem.at[i], rsem.at[i],
                 {"dp": w["dp"], "tm": to})
        dst[h, me] = src[h, me]

    def arrived(dst, h, i):
        wait_bytes(dst.at[h, pl.ds(0, TM - 1)], rsem.at[i])

    regroup(lat, sbl, 0)
    regroup(lat, sbl, 1)
    pl.semaphore_wait(barrier, 41)
    scatter(sbl, rl, 0, 0)
    scatter(sbl, rl, 1, 1)
    regroup(up, sbu, 0)
    regroup(up, sbu, 1)

    def by_pixel(src, dst, h):
        wide = src[h].reshape(512, C).astype(F32)
        for i in range(4):
            t32[i] = wide[:, i * 128:i * 128 + 128]
        for p in range(4):
            for i in range(4):
                dst[pl.ds(h * 512 + p * F, F), i * 128:i * 128 + 128] = (
                    t32[i, pl.ds(p, F, stride=4), :].astype(BF))

    def forward_dense(h):
        base = h * 512
        rows = pl.ds(base, 512)
        by_pixel(rl, x_s, h)
        xx = x_s[rows, :]
        frame = row_of((512, C)) % F
        conv = jnp.where(frame == 0, 0.0, pltpu.roll(nn(xx, wc[0]), 1, 0))
        conv = conv + nn(xx, wc[1])
        conv = conv + jnp.where(frame == F - 1, 0.0, pltpu.roll(nn(xx, wc[2]), 511, 0))
        mid = (xx.astype(F32) + conv).astype(BF)
        mid_s[rows, :] = mid
        upper = mid.astype(F32)
        rinv = lax.rsqrt(jnp.mean(upper * upper, -1, keepdims=True) + 1e-06)
        normed = (upper * rinv * gain[...]).astype(BF)
        nrm_s[rows, :] = normed
        for i, weight in enumerate((wq, wk, wv)):
            qkv_s[rows, i * C:(i + 1) * C] = nn(normed, weight[...]).astype(BF)

    def forward_attend(p):
        rows = pl.ds(pl.multiple_of(p * F, F), F)
        for j in range(4):
            q = qkv_s[rows, j * 128:j * 128 + 128]
            k2 = split_heads(qkv_s[rows, C + j * 128:C + j * 128 + 128])
            v2 = split_heads(qkv_s[rows, 2 * C + j * 128:2 * C + j * 128 + 128])
            s = (nt(k2, q) * 0.125).reshape(2, F, F)
            e = jnp.exp(s - jnp.max(s, 1, keepdims=True))
            probs = (e / jnp.sum(e, 1, keepdims=True)).reshape(2 * F, F)
            pr_s[p * 4 + j] = probs
            att_s[rows, j * 128:j * 128 + 128] = tn(probs.astype(BF), v2).astype(BF)

    for h in range(2):
        arrived(rl, h, h)
        if h == 0:
            scatter(sbu, ru, 0, 2)
        forward_dense(h)
        if h == 1:
            scatter(sbu, ru, 1, 3)

        @pl.loop(4 * h, 4 * h + 4)
        def _(p):
            forward_attend(p)

    def backward_att(h):
        base = h * 512
        rows = pl.ds(base, 512)
        by_pixel(ru, up_s, h)
        da_s[rows, :] = nt(up_s[rows, :], wo[...]).astype(BF)

    def backward_attend(p):
        rows = pl.ds(pl.multiple_of(p * F, F), F)
        for j in range(4):
            lanes = slice(j * 128, j * 128 + 128)
            q = qkv_s[rows, j * 128:j * 128 + 128]
            k2 = split_heads(qkv_s[rows, C + j * 128:C + j * 128 + 128])
            v2 = split_heads(qkv_s[rows, 2 * C + j * 128:2 * C + j * 128 + 128])
            da = da_s[rows, lanes]
            probs = pr_s[p * 4 + j]
            dp = nt(v2, da)
            dv = join_heads(nn(probs.astype(BF), da))
            p3, d3 = probs.reshape(2, F, F), dp.reshape(2, F, F)
            ds = p3 * (d3 - jnp.sum(p3 * d3, 1, keepdims=True)) * 0.125
            ds = ds.reshape(2 * F, F).astype(BF)
            dqkv_s[rows, j * 128:j * 128 + 128] = tn(ds, k2).astype(BF)
            dqkv_s[rows, C + j * 128:C + j * 128 + 128] = join_heads(nn(ds, q)).astype(BF)
            dqkv_s[rows, 2 * C + j * 128:2 * C + j * 128 + 128] = dv.astype(BF)

    def put(i, h, value):
        value = value.reshape(16, 2, 16, C)
        if h == 0:
            g_s[i] = value
        else:
            g_s[i] = g_s[i] + value

    def grads_first(h):
        rows = pl.ds(h * 512, 512)
        put(6, h, tn(att_s[rows, :], up_s[rows, :]))
        for i in range(3):
            put(3 + i, h, tn(nrm_s[rows, :], dqkv_s[rows, i * C:(i + 1) * C]))

    def grads_taps(h):
        rows = pl.ds(h * 512, 512)
        for i in range(3):
            put(i, h, tn(x_s[rows, :], dm_s[rows, i * C:(i + 1) * C]))

    def backward_dense(h):
        base = h * 512
        rows = pl.ds(base, 512)
        d_normed = nt(dqkv_s[rows, 0:C], wq[...])
        d_normed = d_normed + nt(dqkv_s[rows, C:2 * C], wk[...])
        d_normed = d_normed + nt(dqkv_s[rows, 2 * C:3 * C], wv[...])
        upper = mid_s[rows, :].astype(F32)
        rinv = lax.rsqrt(jnp.mean(upper * upper, -1, keepdims=True) + 1e-06)
        term = jnp.sum(d_normed * upper * rinv, 0, keepdims=True)
        if h == 0:
            gain_s[...] = term
        else:
            gain_s[...] = gain_s[...] + term
        scaled = gain[...] * d_normed
        mean = jnp.mean(scaled * upper, -1, keepdims=True)
        d_mid = up_s[rows, :].astype(F32) + rinv * scaled - upper * (rinv * rinv * rinv) * mean
        d_mid = d_mid.astype(BF)
        wide = d_mid.astype(F32)
        frame = row_of((512, C)) % F
        dm_s[rows, 0:C] = jnp.where(frame == F - 1, 0.0, pltpu.roll(wide, 511, 0)).astype(BF)
        dm_s[rows, C:2 * C] = d_mid
        dm_s[rows, 2 * C:3 * C] = jnp.where(frame == 0, 0.0, pltpu.roll(wide, 1, 0)).astype(BF)
        back = nt(dm_s[rows, 0:C], wc[0])
        back = back + nt(dm_s[rows, C:2 * C], wc[1])
        back = back + nt(dm_s[rows, 2 * C:3 * C], wc[2])
        grad = wide + back
        for p in range(4):
            for i in range(4):
                t32[i, pl.ds(p, F, stride=4), :] = (
                    grad[p * F:(p + 1) * F, i * 128:i * 128 + 128])
        for i in range(4):
            osend[h, :, :, i * 128:i * 128 + 128] = t32[i].astype(BF).reshape(TM, 16, 128)

    sib = device(zl, 1 - c, x, y, zh)

    for h in range(2):
        arrived(ru, h, 2 + h)
        backward_att(h)

        @pl.loop(4 * h, 4 * h + 4)
        def _(p):
            backward_attend(p)

        grads_first(h)
        if h == 1:
            for i in range(4):
                g0s_a[:, i] = g_s[3 + i, :, 1 - c].astype(BF)
            send(g0s_a, g0r_a, ssem.at[6], rsem.at[6], sib)
        backward_dense(h)
        scatter(osend, orecv, h, 4 + h)
        grads_taps(h)

    for i in range(3):
        g0s_b[:, i] = g_s[i, :, 1 - c].astype(BF)
    send(g0s_b, g0r_b, ssem.at[7], rsem.at[7], sib)

    gn_s[...] = jnp.concatenate(
        [gain_s[:, i * 128:(i + 1) * 128] for i in range(4)] + [jnp.zeros((4, 128), F32)], 0)
    send(gn_s, gn0, ssem.at[8], rsem.at[8], sib)

    wait_bytes(g0r_a, rsem.at[6])
    for xx in range(4):
        for i in range(4):
            s1_a[xx, :, i] = (
                g_s[3 + i, xx * 4:xx * 4 + 4, c] + g0r_a[xx * 4:xx * 4 + 4, i].astype(F32)
            ).astype(BF)

    @pl.loop(1, 4)
    def _(k):
        to = (x + k) % 4
        send(s1_a.at[to], r1_a.at[x], ssem.at[9], rsem.at[9], device(zl, c, to, y, zh))

    wait_bytes(g0r_b, rsem.at[7])
    for xx in range(4):
        for i in range(3):
            s1_b[:, xx, i] = (
                g_s[i, xx * 4:xx * 4 + 4, c] + g0r_b[xx * 4:xx * 4 + 4, i].astype(F32)
            ).astype(BF)

    @pl.loop(1, 4)
    def _(k):
        to = (y + k) % 4
        send(s1_b.at[to], r1_b.at[y], ssem.at[10], rsem.at[10], device(zl, c, x, to, zh))

    wait_bytes(gn0, rsem.at[8])
    gnx[x] = gn_s[...] + gn0[...]

    @pl.loop(1, 4)
    def _(k):
        to = (x + k) % 4
        send(gnx.at[x], gnx.at[x], ssem.at[11], rsem.at[11], device(zl, c, to, y, zh))

    def total(ref, own, mine):
        acc = own[mine].astype(F32)
        for k in range(1, 4):
            acc = acc + ref[(mine + k) % 4].astype(F32)
        return acc

    wait_bytes(r1_a.at[pl.ds(0, 3)], rsem.at[9])
    s2_a[...] = total(r1_a, s1_a, x).astype(BF)

    @pl.loop(1, 4)
    def _(k):
        to = (y + k) % 4
        send(s2_a.at[to], r2_a.at[y], ssem.at[12], rsem.at[12], device(zl, c, x, to, zh))

    wait_bytes(r1_b.at[pl.ds(0, 3)], rsem.at[10])
    s2_b[...] = total(r1_b, s1_b, y).astype(BF)

    @pl.loop(1, 4)
    def _(k):
        to = (x + k) % 4
        send(s2_b.at[to], r2_b.at[x], ssem.at[13], rsem.at[13], device(zl, c, to, y, zh))

    wait_bytes(gnx.at[pl.ds(0, 3)], rsem.at[11])
    gny[y] = gnx[0] + gnx[1] + gnx[2] + gnx[3]

    @pl.loop(1, 4)
    def _(k):
        to = (y + k) % 4
        send(gny.at[y], gny.at[y], ssem.at[14], rsem.at[14], device(zl, c, x, to, zh))

    wait_bytes(r2_a.at[pl.ds(0, 3)], rsem.at[12])
    ta = total(r2_a, s2_a, y)
    wait_bytes(r2_b.at[pl.ds(0, 3)], rsem.at[13])
    tb = total(r2_b, s2_b, x)
    for q in range(4):
        t_s[q, 0:3] = tb[:, :, q * 128:q * 128 + 128]
        t_s[q, 3:7] = ta[:, :, q * 128:q * 128 + 128]

    wait_bytes(gny.at[pl.ds(0, 3)], rsem.at[14])
    gnz[z] = gny[0] + gny[1] + gny[2] + gny[3]

    @pl.loop(1, 8)
    def _(k):
        send(gnz.at[z], gnz.at[z], ssem.at[15], rsem.at[15], at_z((z + k) % 8, c))

    owner = c == zh

    @pl.loop(0, 4)
    def _(k):
        q = (zl + k) % 4

        @pl.when(jnp.logical_not(jnp.logical_and(owner, k == 0)))
        def _():
            send(t_s.at[q], zr.at[z], ssem.at[16], rsem.at[16], at_z(c * 4 + q, c))

    @pl.when(owner)
    def _():
        zr[z] = t_s[zl]
        wait_bytes(zr.at[pl.ds(0, 7)], rsem.at[16])
        acc = zr[0]
        for k in range(1, 8):
            acc = acc + zr[k]
        agr[zl] = acc

        @pl.loop(1, 8)
        def _(k):
            to = (zl * 2 + c + k) % 8
            send(agr.at[zl], agr.at[zl], ssem.at[17], rsem.at[17],
                 at_z(zh * 4 + to // 2, to % 2))

        wait_bytes(agr.at[pl.ds(0, 3)], rsem.at[17])

    @pl.when(jnp.logical_not(owner))
    def _():
        wait_bytes(agr, rsem.at[17])

    for q in range(4):
        ograds[:, :, q * 128:q * 128 + 128] = agr[q]

    wait_bytes(gnz.at[pl.ds(0, 7)], rsem.at[15])
    acc = gnz[0]
    for k in range(1, 8):
        acc = acc + gnz[k]
    ogain[...] = acc

    low = row_of((F, C)) % 8 < 4
    for h in range(2):
        arrived(orecv, h, 4 + h)
        got = [[], [], [], []]
        for m in range(16):
            for o in range(2):
                tile = orecv[h, 2 * m + o].astype(F32)
                got[o].append(tile[0:8])
                got[2 + o].append(tile[8:16])
        got = [jnp.concatenate(g, 0) for g in got]
        for f in (0, 2):
            even, odd = got[f], got[f + 1]
            out[f, 128 * h:128 * h + 128, :] = jnp.where(
                low, even, pltpu.roll(odd, 4, 0)).astype(BF)
            out[f + 1, 128 * h:128 * h + 128, :] = jnp.where(
                low, pltpu.roll(even, F - 4, 0), odd).astype(BF)

    for i, ref in enumerate((sbl, sbl, sbu, sbu, osend, osend)):
        wait_bytes(ref.at[i % 2, pl.ds(0, TM - 1)], ssem.at[i])
    wait_bytes(g0s_a, ssem.at[6])
    wait_bytes(g0s_b, ssem.at[7])
    wait_bytes(gn_s, ssem.at[8])
    wait_bytes(s1_a.at[pl.ds(0, 3)], ssem.at[9])
    wait_bytes(s1_b.at[pl.ds(0, 3)], ssem.at[10])
    wait_bytes(gnx.at[pl.ds(0, 3)], ssem.at[11])
    wait_bytes(s2_a.at[pl.ds(0, 3)], ssem.at[12])
    wait_bytes(s2_b.at[pl.ds(0, 3)], ssem.at[13])
    wait_bytes(gny.at[pl.ds(0, 3)], ssem.at[14])
    wait_bytes(gnz.at[pl.ds(0, 7)], ssem.at[15])

    @pl.when(owner)
    def _():
        wait_bytes(t_s.at[pl.ds(0, 3)], ssem.at[16])
        wait_bytes(zr.at[pl.ds(0, 7)], ssem.at[17])

    @pl.when(jnp.logical_not(owner))
    def _():
        wait_bytes(t_s, ssem.at[16])


def block(latents, upstream, conv_weight, w_query, w_key, w_value, w_out, norm_gain):
    v = lambda shape, dtype=BF: pltpu.VMEM(shape, dtype)
    scratch = [
        v((2, TM, 16, C)), v((2, TM, 16, C)), v((2, TM, 16, C)), v((2, TM, 16, C)),
        v((2, TM, 16, C)), v((2, TM, 16, C)),
        v((4, 512, 128), F32), v((1024, C)), v((1024, C)), v((1024, C)), v((1024, 3 * C)),
        v((32, 256, F), F32), v((1024, C)), v((1024, C)), v((1024, C)),
        v((1024, 3 * C)), v((1024, 3 * C)),
        v((7, 16, 2, 16, C), F32), v((1, C), F32),
        v((16, 4, 16, C)), v((16, 3, 16, C)), v((16, 4, 16, C)), v((16, 3, 16, C)),
        v((4, 4, 4, 16, C)), v((4, 4, 4, 16, C)), v((4, 4, 16, C)), v((4, 4, 16, C)),
        v((4, 4, 3, 16, C)), v((4, 4, 3, 16, C)), v((4, 3, 16, C)), v((4, 3, 16, C)),
        v((4, 7, 16, 128), F32), v((8, 7, 16, 128), F32), v((7, 16, 128), F32),
        v((4, 7, 16, 128), F32),
        v((8, 128), F32), v((8, 128), F32), v((4, 8, 128), F32), v((4, 8, 128), F32),
        v((8, 8, 128), F32),
        pltpu.SemaphoreType.DMA((18,)), pltpu.SemaphoreType.DMA((18,)),
    ]
    vmem = pl.BlockSpec(memory_space=pltpu.VMEM)
    return pl.pallas_call(
        kernel,
        out_shape=(
            jax.ShapeDtypeStruct((4, 256, C), BF),
            jax.ShapeDtypeStruct((7, 16, C), F32),
            jax.ShapeDtypeStruct((8, 128), F32),
        ),
        in_specs=[vmem] * 8,
        out_specs=(vmem, vmem, vmem),
        scratch_shapes=scratch,
        compiler_params=pltpu.CompilerParams(
            collective_id=0, has_side_effects=True, vmem_limit_bytes=60 * 2**20
        ),
        name="block_backward",
    )(latents, upstream, conv_weight, w_query, w_key, w_value, w_out, norm_gain)


def per_device(latents, upstream, conv_weight, w_query, w_key, w_value, w_out, norm_gain):
    grad_in, rows, gain_rows = block(
        latents[0], upstream[0], conv_weight, w_query, w_key, w_value, w_out, norm_gain[None]
    )
    gain_rows = lax.dynamic_slice(
        gain_rows.reshape(-1), (lax.axis_index("tm") * 16,), (16,))
    return (grad_in[None], rows[0:3], rows[3], rows[4], rows[5], rows[6], gain_rows)


def solution(mesh):
    return jax.shard_map(
        per_device,
        mesh=mesh,
        in_specs=(P("dp", "tm", None, None), P("dp", "tm", None, None),
                  P(), P(), P(), P(), P(), P()),
        out_specs=(
            P("dp", "tm", None, None),
            P(None, "tm", None),
            P("tm", None),
            P("tm", None),
            P("tm", None),
            P("tm", None),
            P("tm"),
        ),
        check_vma=False,
    )
```

```python
import jax
import jax.numpy as jnp
from jax import lax
from jax.experimental import pallas as pl
from jax.experimental.pallas import tpu as pltpu
from jax.sharding import PartitionSpec as P

C = 512
F = 128
TM = 32
BF = jnp.bfloat16
F32 = jnp.float32
MESH_ID = pl.DeviceIdType.MESH


def nn(a, b):
    return lax.dot_general(a, b, (((1,), (0,)), ((), ())), preferred_element_type=F32)


def nt(a, b):
    return lax.dot_general(a, b, (((1,), (1,)), ((), ())), preferred_element_type=F32)


def tn(a, b):
    return lax.dot_general(a, b, (((0,), (0,)), ((), ())), preferred_element_type=F32)


def where_am_i():
    dp, tm = lax.axis_index("dp"), lax.axis_index("tm")
    return dict(dp=dp, tm=tm, zl=dp // 2, c=dp % 2, x=tm // 8, y=(tm // 2) % 4, zh=tm % 2)


def device(zl, c, x, y, zh):
    return {"dp": zl * 2 + c, "tm": (x * 4 + y) * 2 + zh}


def signal(sem, dev):
    pl.semaphore_signal(sem, inc=1, device_id=dev, device_id_type=MESH_ID)


def send(src, dst, ssem, rsem, dev):
    pltpu.make_async_remote_copy(
        src_ref=src, dst_ref=dst, send_sem=ssem, recv_sem=rsem,
        device_id=dev, device_id_type=MESH_ID,
    ).start()


def wait_bytes(ref, sem):
    pltpu.make_async_copy(ref, ref, sem).wait()


def row_of(shape):
    return lax.broadcasted_iota(jnp.int32, shape, 0)


def split_heads(a):
    lane = lax.broadcasted_iota(jnp.int32, a.shape, 1)
    zero = jnp.zeros_like(a)
    return jnp.concatenate([jnp.where(lane < 64, a, zero), jnp.where(lane < 64, zero, a)], 0)


def join_heads(a):
    lane = lax.broadcasted_iota(jnp.int32, (F, 128), 1)
    return jnp.where(lane < 64, a[:F], a[F:])


GROUPS = ((6,), (3, 4, 5), (0, 1, 2))


def kernel(
    lat_in, up_in, wc_in, wq_in, wk_in, wv_in, wo_in, gain,
    orecv, og0, og1, og2, ogain,
    lat, up, wc, wq, wk, wv, wo,
    sbl, sbu, rl, ru, osend,
    t32, x_s, mid_s, nrm_s, qkv_s, pr_s, att_s, up_s, da_s, dqkv_s, dm_s,
    g_s, gain_s, gn_s, gn0, gnx, gny, gnz,
    *rest,
):
    ssem, rsem, lsem = rest[-3:]
    red = [dict(zip(("g0s", "g0r", "s1x", "r1x", "s1y", "r1y", "s2x", "r2x", "s2y", "r2y",
                     "ts", "zr"), rest[12 * i:12 * i + 12])) for i in range(3)]
    agr = (og0, og1, og2)
    loads = [
        pltpu.make_async_copy(src, dst, lsem.at[i])
        for i, (src, dst) in enumerate(
            ((lat_in, lat), (up_in, up), (wc_in, wc), (wq_in, wq), (wk_in, wk),
             (wv_in, wv), (wo_in, wo)))
    ]
    for load in loads:
        load.start()
    w = where_am_i()
    me, c, x, y, zl, zh = w["tm"], w["c"], w["x"], w["y"], w["zl"], w["zh"]
    z = zh * 4 + zl

    def at_z(zz, cc):
        return device(zz % 4, cc, x, y, zz // 4)

    barrier = pltpu.get_barrier_semaphore()

    @pl.loop(1, TM)
    def _(k):
        signal(barrier, {"dp": w["dp"], "tm": (me + k) % TM})

    signal(barrier, device(zl, 1 - c, x, y, zh))

    @pl.loop(1, 8)
    def _(k):
        @pl.when(k != 4)
        def _():
            signal(barrier, at_z((z + k) % 8, c))

    @pl.loop(1, 4)
    def _(k):
        signal(barrier, at_z(zh * 4 + (zl + k) % 4, 1 - c))

    def regroup(src, dst, h):
        a = [src[f, 128 * h:128 * h + 128, :].astype(F32) for f in range(4)]
        low = row_of((F, C)) % 8 < 4
        tiles = []
        for f in (0, 2):
            even = jnp.where(low, a[f], pltpu.roll(a[f + 1], 4, 0))
            odd = jnp.where(low, pltpu.roll(a[f], F - 4, 0), a[f + 1])
            tiles.append((even.reshape(16, 8, C), odd.reshape(16, 8, C)))
        for m in range(16):
            for o in range(2):
                dst[h, 2 * m + o] = jnp.concatenate(
                    [tiles[0][o][m], tiles[1][o][m]], 0
                ).astype(BF)

    def scatter(src, dst, h, i):
        @pl.loop(1, TM)
        def _(k):
            to = (me + k) % TM
            send(src.at[h, to], dst.at[h, me], ssem.at[i], rsem.at[i],
                 {"dp": w["dp"], "tm": to})

    def arrived(dst, h, i):
        wait_bytes(dst.at[h, pl.ds(0, TM - 1)], rsem.at[i])

    loads[0].wait()
    regroup(lat, sbl, 0)
    regroup(lat, sbl, 1)
    pl.semaphore_wait(barrier, 41)
    scatter(sbl, rl, 0, 0)
    scatter(sbl, rl, 1, 1)
    for h in range(2):
        rl[h, me] = sbl[h, me]
    loads[1].wait()
    regroup(up, sbu, 0)
    regroup(up, sbu, 1)
    for h in range(2):
        ru[h, me] = sbu[h, me]
    for load in loads[2:]:
        load.wait()

    def by_pixel(src, dst, h):
        wide = src[h].reshape(512, C).astype(F32)
        for i in range(4):
            t32[i] = wide[:, i * 128:i * 128 + 128]
        for p in range(4):
            for i in range(4):
                dst[pl.ds(h * 512 + p * F, F), i * 128:i * 128 + 128] = (
                    t32[i, pl.ds(p, F, stride=4), :].astype(BF))

    def forward_dense(h):
        base = h * 512
        rows = pl.ds(base, 512)
        by_pixel(rl, x_s, h)
        xx = x_s[rows, :]
        frame = row_of((512, C)) % F
        conv = jnp.where(frame == 0, 0.0, pltpu.roll(nn(xx, wc[0]), 1, 0))
        conv = conv + nn(xx, wc[1])
        conv = conv + jnp.where(frame == F - 1, 0.0, pltpu.roll(nn(xx, wc[2]), 511, 0))
        mid = (xx.astype(F32) + conv).astype(BF)
        mid_s[rows, :] = mid
        upper = mid.astype(F32)
        rinv = lax.rsqrt(jnp.mean(upper * upper, -1, keepdims=True) + 1e-06)
        normed = (upper * rinv * gain[...]).astype(BF)
        nrm_s[rows, :] = normed
        for i, weight in enumerate((wq, wk, wv)):
            qkv_s[rows, i * C:(i + 1) * C] = nn(normed, weight[...]).astype(BF)

    def forward_attend(p):
        rows = pl.ds(pl.multiple_of(p * F, F), F)
        for j in range(4):
            q = qkv_s[rows, j * 128:j * 128 + 128]
            k2 = split_heads(qkv_s[rows, C + j * 128:C + j * 128 + 128])
            v2 = split_heads(qkv_s[rows, 2 * C + j * 128:2 * C + j * 128 + 128])
            s = (nt(k2, q) * 0.125).reshape(2, F, F)
            e = jnp.exp(s - jnp.max(s, 1, keepdims=True))
            probs = (e / jnp.sum(e, 1, keepdims=True)).reshape(2 * F, F)
            pr_s[p * 4 + j] = probs
            att_s[rows, j * 128:j * 128 + 128] = tn(probs.astype(BF), v2).astype(BF)

    for h in range(2):
        arrived(rl, h, h)
        if h == 0:
            scatter(sbu, ru, 0, 2)
        forward_dense(h)
        if h == 1:
            scatter(sbu, ru, 1, 3)

        @pl.loop(4 * h, 4 * h + 4)
        def _(p):
            forward_attend(p)

    def backward_att(h):
        base = h * 512
        rows = pl.ds(base, 512)
        by_pixel(ru, up_s, h)
        da_s[rows, :] = nt(up_s[rows, :], wo[...]).astype(BF)

    def backward_attend(p):
        rows = pl.ds(pl.multiple_of(p * F, F), F)
        for j in range(4):
            lanes = slice(j * 128, j * 128 + 128)
            q = qkv_s[rows, j * 128:j * 128 + 128]
            k2 = split_heads(qkv_s[rows, C + j * 128:C + j * 128 + 128])
            v2 = split_heads(qkv_s[rows, 2 * C + j * 128:2 * C + j * 128 + 128])
            da = da_s[rows, lanes]
            probs = pr_s[p * 4 + j]
            dp = nt(v2, da)
            dv = join_heads(nn(probs.astype(BF), da))
            p3, d3 = probs.reshape(2, F, F), dp.reshape(2, F, F)
            ds = p3 * (d3 - jnp.sum(p3 * d3, 1, keepdims=True)) * 0.125
            ds = ds.reshape(2 * F, F).astype(BF)
            dqkv_s[rows, j * 128:j * 128 + 128] = tn(ds, k2).astype(BF)
            dqkv_s[rows, C + j * 128:C + j * 128 + 128] = join_heads(nn(ds, q)).astype(BF)
            dqkv_s[rows, 2 * C + j * 128:2 * C + j * 128 + 128] = dv.astype(BF)

    def put(i, h, value):
        value = value.reshape(16, 2, 16, C)
        if h == 0:
            g_s[i] = value
        else:
            g_s[i] = g_s[i] + value

    def grads_out(h):
        rows = pl.ds(h * 512, 512)
        put(6, h, tn(att_s[rows, :], up_s[rows, :]))

    def grads_first(h):
        rows = pl.ds(h * 512, 512)
        for i in range(3):
            put(3 + i, h, tn(nrm_s[rows, :], dqkv_s[rows, i * C:(i + 1) * C]))

    def grads_taps(h):
        rows = pl.ds(h * 512, 512)
        for i in range(3):
            put(i, h, tn(x_s[rows, :], dm_s[rows, i * C:(i + 1) * C]))

    def backward_dense(h):
        base = h * 512
        rows = pl.ds(base, 512)
        d_normed = nt(dqkv_s[rows, 0:C], wq[...])
        d_normed = d_normed + nt(dqkv_s[rows, C:2 * C], wk[...])
        d_normed = d_normed + nt(dqkv_s[rows, 2 * C:3 * C], wv[...])
        upper = mid_s[rows, :].astype(F32)
        rinv = lax.rsqrt(jnp.mean(upper * upper, -1, keepdims=True) + 1e-06)
        term = jnp.sum(d_normed * upper * rinv, 0, keepdims=True)
        if h == 0:
            gain_s[...] = term
        else:
            gain_s[...] = gain_s[...] + term
        scaled = gain[...] * d_normed
        mean = jnp.mean(scaled * upper, -1, keepdims=True)
        d_mid = up_s[rows, :].astype(F32) + rinv * scaled - upper * (rinv * rinv * rinv) * mean
        d_mid = d_mid.astype(BF)
        wide = d_mid.astype(F32)
        frame = row_of((512, C)) % F
        dm_s[rows, 0:C] = jnp.where(frame == F - 1, 0.0, pltpu.roll(wide, 511, 0)).astype(BF)
        dm_s[rows, C:2 * C] = d_mid
        dm_s[rows, 2 * C:3 * C] = jnp.where(frame == 0, 0.0, pltpu.roll(wide, 1, 0)).astype(BF)
        back = nt(dm_s[rows, 0:C], wc[0])
        back = back + nt(dm_s[rows, C:2 * C], wc[1])
        back = back + nt(dm_s[rows, 2 * C:3 * C], wc[2])
        grad = wide + back
        for p in range(4):
            for i in range(4):
                t32[i, pl.ds(p, F, stride=4), :] = (
                    grad[p * F:(p + 1) * F, i * 128:i * 128 + 128])
        for i in range(4):
            osend[h, :, :, i * 128:i * 128 + 128] = t32[i].astype(BF).reshape(TM, 16, 128)

    sib = device(zl, 1 - c, x, y, zh)
    owner = c == zh
    not_owner = jnp.logical_not(owner)

    def to_x(to):
        return device(zl, c, to, y, zh)

    def to_y(to):
        return device(zl, c, x, to, zh)

    def red_cores(g):
        r = red[g]
        for i, m in enumerate(GROUPS[g]):
            r["g0s"][:, i] = g_s[m, :, 1 - c].astype(BF)
        send(r["g0s"], r["g0r"], ssem.at[6 + 7 * g], rsem.at[6 + 7 * g], sib)

    def red_first(g):
        r, s = red[g], 7 + 7 * g
        wait_bytes(r["g0r"], rsem.at[6 + 7 * g])
        for i, m in enumerate(GROUPS[g]):
            for xx in range(4):
                four = slice(xx * 4, xx * 4 + 4)
                both = g_s[m, four, c] + r["g0r"][four, i].astype(F32)
                r["s1x"][xx, :, i] = both[:, :, :256].astype(BF)
                r["s1y"][:, xx, i] = both[:, :, 256:].astype(BF)

        @pl.loop(1, 4)
        def _(k):
            tx, ty = (x + k) % 4, (y + k) % 4
            send(r["s1x"].at[tx], r["r1x"].at[x], ssem.at[s], rsem.at[s], to_x(tx))
            send(r["s1y"].at[ty], r["r1y"].at[y], ssem.at[s + 1], rsem.at[s + 1], to_y(ty))

    def total(ref, own, mine):
        acc = own[mine].astype(F32)
        for k in range(1, 4):
            acc = acc + ref[(mine + k) % 4].astype(F32)
        return acc

    def red_second(g):
        r, s = red[g], 7 + 7 * g
        wait_bytes(r["r1x"].at[pl.ds(0, 3)], rsem.at[s])
        r["s2x"][...] = total(r["r1x"], r["s1x"], x).astype(BF)

        @pl.loop(1, 4)
        def _(k):
            ty = (y + k) % 4
            send(r["s2x"].at[ty], r["r2x"].at[y], ssem.at[s + 2], rsem.at[s + 2], to_y(ty))

        wait_bytes(r["r1y"].at[pl.ds(0, 3)], rsem.at[s + 1])
        r["s2y"][...] = total(r["r1y"], r["s1y"], y).astype(BF)

        @pl.loop(1, 4)
        def _(k):
            tx = (x + k) % 4
            send(r["s2y"].at[tx], r["r2y"].at[x], ssem.at[s + 3], rsem.at[s + 3], to_x(tx))

    def red_z(g):
        r, s = red[g], 7 + 7 * g
        wait_bytes(r["r2x"].at[pl.ds(0, 3)], rsem.at[s + 2])
        half = total(r["r2x"], r["s2x"], y).astype(BF)
        r["ts"][0] = half[:, :, :128]
        r["ts"][1] = half[:, :, 128:]
        wait_bytes(r["r2y"].at[pl.ds(0, 3)], rsem.at[s + 3])
        half = total(r["r2y"], r["s2y"], x).astype(BF)
        r["ts"][2] = half[:, :, :128]
        r["ts"][3] = half[:, :, 128:]

        @pl.loop(0, 4)
        def _(k):
            q = (zl + k) % 4

            @pl.when(jnp.logical_or(not_owner, k != 0))
            def _():
                send(r["ts"].at[q], r["zr"].at[z], ssem.at[s + 4], rsem.at[s + 4],
                     at_z(c * 4 + q, c))

    def red_gather(g):
        r, s = red[g], 7 + 7 * g

        @pl.when(owner)
        def _():
            r["zr"][z] = r["ts"][zl]
            wait_bytes(r["zr"].at[pl.ds(0, 7)], rsem.at[s + 4])
            acc = r["zr"][0].astype(F32)
            for k in range(1, 8):
                acc = acc + r["zr"][k].astype(F32)
            agr[g][zl] = acc.astype(BF)

            @pl.loop(1, 8)
            def _(k):
                to = (zl * 2 + c + k) % 8
                send(agr[g].at[zl], agr[g].at[zl], ssem.at[s + 5], rsem.at[s + 5],
                     at_z(zh * 4 + to // 2, to % 2))

    def red_end(g):
        r, s = red[g], 7 + 7 * g

        @pl.when(owner)
        def _():
            wait_bytes(agr[g].at[pl.ds(0, 3)], rsem.at[s + 5])
            wait_bytes(r["ts"].at[pl.ds(0, 3)], ssem.at[s + 4])
            wait_bytes(r["zr"].at[pl.ds(0, 7)], ssem.at[s + 5])

        @pl.when(not_owner)
        def _():
            wait_bytes(agr[g], rsem.at[s + 5])
            wait_bytes(r["ts"], ssem.at[s + 4])

        wait_bytes(r["g0s"], ssem.at[6 + 7 * g])
        wait_bytes(r["s1x"].at[pl.ds(0, 3)], ssem.at[s])
        wait_bytes(r["s1y"].at[pl.ds(0, 3)], ssem.at[s + 1])
        wait_bytes(r["s2x"].at[pl.ds(0, 3)], ssem.at[s + 2])
        wait_bytes(r["s2y"].at[pl.ds(0, 3)], ssem.at[s + 3])

    def gain_cores():
        gn_s[...] = jnp.concatenate(
            [gain_s[:, i * 128:(i + 1) * 128] for i in range(4)] + [jnp.zeros((4, 128), F32)], 0)
        send(gn_s, gn0, ssem.at[27], rsem.at[27], sib)

    def gain_x():
        wait_bytes(gn0, rsem.at[27])
        gnx[x] = gn_s[...] + gn0[...]

        @pl.loop(1, 4)
        def _(k):
            send(gnx.at[x], gnx.at[x], ssem.at[28], rsem.at[28], to_x((x + k) % 4))

    def gain_y():
        wait_bytes(gnx.at[pl.ds(0, 3)], rsem.at[28])
        gny[y] = gnx[0] + gnx[1] + gnx[2] + gnx[3]

        @pl.loop(1, 4)
        def _(k):
            send(gny.at[y], gny.at[y], ssem.at[29], rsem.at[29], to_y((y + k) % 4))

    def gain_z():
        wait_bytes(gny.at[pl.ds(0, 3)], rsem.at[29])
        gnz[z] = gny[0] + gny[1] + gny[2] + gny[3]

        @pl.loop(1, 8)
        def _(k):
            send(gnz.at[z], gnz.at[z], ssem.at[30], rsem.at[30], at_z((z + k) % 8, c))

    def gain_end():
        wait_bytes(gnz.at[pl.ds(0, 7)], rsem.at[30])
        acc = gnz[0]
        for k in range(1, 8):
            acc = acc + gnz[k]
        ogain[...] = acc
        wait_bytes(gn_s, ssem.at[27])
        wait_bytes(gnx.at[pl.ds(0, 3)], ssem.at[28])
        wait_bytes(gny.at[pl.ds(0, 3)], ssem.at[29])
        wait_bytes(gnz.at[pl.ds(0, 7)], ssem.at[30])

    own_out = [pltpu.make_async_copy(osend.at[h, me], orecv.at[h, me], lsem.at[7 + h])
               for h in range(2)]

    arrived(ru, 0, 2)
    backward_att(0)

    @pl.loop(0, 4)
    def _(p):
        backward_attend(p)

    grads_out(0)
    grads_first(0)
    backward_dense(0)
    grads_taps(0)
    scatter(osend, orecv, 0, 4)
    own_out[0].start()

    arrived(ru, 1, 3)
    backward_att(1)
    grads_out(1)
    red_cores(0)

    @pl.loop(4, 6)
    def _(p):
        backward_attend(p)

    red_first(0)

    @pl.loop(6, 8)
    def _(p):
        backward_attend(p)

    grads_first(1)
    red_cores(1)
    red_second(0)
    backward_dense(1)
    red_first(1)
    gain_cores()
    scatter(osend, orecv, 1, 5)
    own_out[1].start()
    grads_taps(1)
    red_cores(2)
    red_z(0)
    gain_x()
    red_first(2)
    red_gather(0)
    red_second(1)
    gain_y()
    red_second(2)
    red_z(1)
    gain_z()
    red_z(2)
    red_gather(1)
    red_gather(2)
    for g in range(3):
        red_end(g)
    gain_end()

    for h in range(2):
        arrived(orecv, h, 4 + h)
        own_out[h].wait()
    for i, ref in enumerate((sbl, sbl, sbu, sbu, osend, osend)):
        wait_bytes(ref.at[i % 2, pl.ds(0, TM - 1)], ssem.at[i])


def finish(orecv, og0, og1, og2, ogain, out, conv, query, key, value, outer, gain):
    low = row_of((F, C)) % 8 < 4
    for h in range(2):
        got = [[], [], [], []]
        for m in range(16):
            for o in range(2):
                tile = orecv[h, 2 * m + o].astype(F32)
                got[o].append(tile[0:8])
                got[2 + o].append(tile[8:16])
        got = [jnp.concatenate(g, 0) for g in got]
        for f in (0, 2):
            even, odd = got[f], got[f + 1]
            out[f, 128 * h:128 * h + 128, :] = jnp.where(
                low, even, pltpu.roll(odd, 4, 0)).astype(BF)
            out[f + 1, 128 * h:128 * h + 128, :] = jnp.where(
                low, pltpu.roll(even, F - 4, 0), odd).astype(BF)
    for q in range(4):
        lanes = slice(q * 128, q * 128 + 128)
        outer[:, lanes] = og0[q, 0].astype(F32)
        for i, ref in enumerate((query, key, value)):
            ref[:, lanes] = og1[q, i].astype(F32)
        conv[:, :, lanes] = og2[q].astype(F32)
    tm = lax.axis_index("tm")
    row = ogain[pl.ds(tm // 8, 1), :]
    gain[...] = pltpu.roll(row, (128 - (tm % 8) * 16) % 128, 1)[0, :16]


def block(latents, upstream, conv_weight, w_query, w_key, w_value, w_out, norm_gain):
    v = lambda shape, dtype=BF: pltpu.VMEM(shape, dtype)
    scratch = [
        v((4, 256, C)), v((4, 256, C)), v((3, C, C)), v((C, C)), v((C, C)), v((C, C)), v((C, C)),
        v((2, TM, 16, C)), v((2, TM, 16, C)), v((2, TM, 16, C)), v((2, TM, 16, C)),
        v((2, TM, 16, C)),
        v((4, 512, 128), F32), v((1024, C)), v((1024, C)), v((1024, C)), v((1024, 3 * C)),
        v((32, 256, F), F32), v((1024, C)), v((1024, C)), v((1024, C)),
        v((1024, 3 * C)), v((1024, 3 * C)),
        v((7, 16, 2, 16, C), F32), v((1, C), F32),
        v((8, 128), F32), v((8, 128), F32), v((4, 8, 128), F32), v((4, 8, 128), F32),
        v((8, 8, 128), F32),
    ]
    for group in GROUPS:
        n = len(group)
        scratch += [v((16, n, 16, C))] * 2 + [v((4, 4, n, 16, 256))] * 4
        scratch += [v((4, n, 16, 256))] * 4 + [v((4, n, 16, 128)), v((8, n, 16, 128))]
    scratch += [pltpu.SemaphoreType.DMA((31,)), pltpu.SemaphoreType.DMA((31,)),
                pltpu.SemaphoreType.DMA((9,))]
    vmem = pl.BlockSpec(memory_space=pltpu.VMEM)
    hbm = pl.BlockSpec(memory_space=pl.ANY)
    got = pl.pallas_call(
        kernel,
        out_shape=(
            jax.ShapeDtypeStruct((2, TM, 16, C), BF),
            jax.ShapeDtypeStruct((4, 1, 16, 128), BF),
            jax.ShapeDtypeStruct((4, 3, 16, 128), BF),
            jax.ShapeDtypeStruct((4, 3, 16, 128), BF),
            jax.ShapeDtypeStruct((8, 128), F32),
        ),
        in_specs=[hbm] * 7 + [vmem],
        out_specs=(hbm, vmem, vmem, vmem, vmem),
        scratch_shapes=scratch,
        compiler_params=pltpu.CompilerParams(
            collective_id=0, has_side_effects=True, vmem_limit_bytes=60 * 2**20
        ),
        name="block_backward",
    )(latents, upstream, conv_weight, w_query, w_key, w_value, w_out, norm_gain)
    rows = jax.ShapeDtypeStruct((16, C), F32)
    return pl.pallas_call(
        finish,
        out_shape=(
            jax.ShapeDtypeStruct((4, 256, C), BF),
            jax.ShapeDtypeStruct((3, 16, C), F32),
            rows, rows, rows, rows,
            jax.ShapeDtypeStruct((16,), F32),
        ),
        in_specs=[vmem] * 5,
        out_specs=(vmem,) * 7,
        name="finish",
    )(*got)


def per_device(latents, upstream, conv_weight, w_query, w_key, w_value, w_out, norm_gain):
    grad_in, *grads = block(
        latents[0], upstream[0], conv_weight, w_query, w_key, w_value, w_out, norm_gain[None]
    )
    return (grad_in[None], *grads)


def solution(mesh):
    return jax.shard_map(
        per_device,
        mesh=mesh,
        in_specs=(P("dp", "tm", None, None), P("dp", "tm", None, None),
                  P(), P(), P(), P(), P(), P()),
        out_specs=(
            P("dp", "tm", None, None),
            P(None, "tm", None),
            P("tm", None),
            P("tm", None),
            P("tm", None),
            P("tm", None),
            P("tm"),
        ),
        check_vma=False,
    )
```

```python
import jax
import jax.numpy as jnp
from jax import lax
from jax.experimental import pallas as pl
from jax.experimental.pallas import tpu as pltpu
from jax.sharding import PartitionSpec as P

C = 512
F = 128
TM = 32
BF = jnp.bfloat16
F32 = jnp.float32
MESH_ID = pl.DeviceIdType.MESH


def nn(a, b):
    return lax.dot_general(a, b, (((1,), (0,)), ((), ())), preferred_element_type=F32)


def nt(a, b):
    return lax.dot_general(a, b, (((1,), (1,)), ((), ())), preferred_element_type=F32)


def tn(a, b):
    return lax.dot_general(a, b, (((0,), (0,)), ((), ())), preferred_element_type=F32)


def where_am_i():
    dp, tm = lax.axis_index("dp"), lax.axis_index("tm")
    return dict(dp=dp, tm=tm, zl=dp // 2, c=dp % 2, x=tm // 8, y=(tm // 2) % 4, zh=tm % 2)


def device(zl, c, x, y, zh):
    return {"dp": zl * 2 + c, "tm": (x * 4 + y) * 2 + zh}


def signal(sem, dev):
    pl.semaphore_signal(sem, inc=1, device_id=dev, device_id_type=MESH_ID)


def send(src, dst, ssem, rsem, dev):
    pltpu.make_async_remote_copy(
        src_ref=src, dst_ref=dst, send_sem=ssem, recv_sem=rsem,
        device_id=dev, device_id_type=MESH_ID,
    ).start()


def wait_bytes(ref, sem):
    pltpu.make_async_copy(ref, ref, sem).wait()


def row_of(shape):
    return lax.broadcasted_iota(jnp.int32, shape, 0)


def split_heads(a):
    lane = lax.broadcasted_iota(jnp.int32, a.shape, 1)
    zero = jnp.zeros_like(a)
    return jnp.concatenate([jnp.where(lane < 64, a, zero), jnp.where(lane < 64, zero, a)], 0)


def join_heads(a):
    lane = lax.broadcasted_iota(jnp.int32, (F, 128), 1)
    return jnp.where(lane < 64, a[:F], a[F:])


GROUPS = ((6, 5), (3, 4), (0,), (1,), (2,))
NG = len(GROUPS)
GS = 6 + 7 * NG


def kernel(
    lat_in, up_in, wc_in, wq_in, wk_in, wv_in, wo_in, gain,
    orecv, og0, og1, og2, og3, og4, ogain,
    lat, up, wc, wq, wk, wv, wo,
    sbl, sbu, rl, ru, osend,
    t32, x_s, mid_s, nt_s, xt_s, at_s, qkv_s, pr_s, up_s, da_s, dqkv_s, dm_s,
    g_s, gain_s, gn_s, gn0, gnx, gny, gnz,
    *rest,
):
    ssem, rsem, lsem = rest[-3:]
    red = [dict(zip(("g0s", "g0r", "s1x", "r1x", "s1y", "r1y", "s2x", "r2x", "s2y", "r2y",
                     "ts", "zr"), rest[12 * i:12 * i + 12])) for i in range(NG)]
    agr = (og0, og1, og2, og3, og4)
    loads = [
        pltpu.make_async_copy(src, dst, lsem.at[i])
        for i, (src, dst) in enumerate(
            ((lat_in, lat), (up_in, up), (wc_in, wc), (wq_in, wq), (wk_in, wk),
             (wv_in, wv), (wo_in, wo)))
    ]
    for load in loads:
        load.start()
    w = where_am_i()
    me, c, x, y, zl, zh = w["tm"], w["c"], w["x"], w["y"], w["zl"], w["zh"]
    z = zh * 4 + zl

    def at_z(zz, cc):
        return device(zz % 4, cc, x, y, zz // 4)

    barrier = pltpu.get_barrier_semaphore()

    @pl.loop(1, TM)
    def _(k):
        signal(barrier, {"dp": w["dp"], "tm": (me + k) % TM})

    signal(barrier, device(zl, 1 - c, x, y, zh))

    @pl.loop(1, 8)
    def _(k):
        @pl.when(k != 4)
        def _():
            signal(barrier, at_z((z + k) % 8, c))

    @pl.loop(1, 4)
    def _(k):
        signal(barrier, at_z(zh * 4 + (zl + k) % 4, 1 - c))

    def regroup(src, dst, h):
        a = [src[f, 128 * h:128 * h + 128, :].astype(F32) for f in range(4)]
        low = row_of((F, C)) % 8 < 4
        tiles = []
        for f in (0, 2):
            even = jnp.where(low, a[f], pltpu.roll(a[f + 1], 4, 0))
            odd = jnp.where(low, pltpu.roll(a[f], F - 4, 0), a[f + 1])
            tiles.append((even.reshape(16, 8, C), odd.reshape(16, 8, C)))
        for m in range(16):
            for o in range(2):
                dst[h, 2 * m + o] = jnp.concatenate(
                    [tiles[0][o][m], tiles[1][o][m]], 0
                ).astype(BF)

    def scatter(src, dst, h, i, lo=1, hi=TM):
        @pl.loop(lo, hi)
        def _(k):
            to = (me + k) % TM
            send(src.at[h, to], dst.at[h, me], ssem.at[i], rsem.at[i],
                 {"dp": w["dp"], "tm": to})

    def arrived(dst, h, i):
        wait_bytes(dst.at[h, pl.ds(0, TM - 1)], rsem.at[i])

    loads[0].wait()
    regroup(lat, sbl, 0)
    regroup(lat, sbl, 1)
    pl.semaphore_wait(barrier, 41)
    scatter(sbl, rl, 0, 0)
    scatter(sbl, rl, 1, 1)
    for h in range(2):
        rl[h, me] = sbl[h, me]
    loads[1].wait()
    regroup(up, sbu, 0)
    regroup(up, sbu, 1)
    for h in range(2):
        ru[h, me] = sbu[h, me]
    for load in loads[2:]:
        load.wait()

    def by_pixel(src, dst, h):
        wide = src[h].reshape(512, C).astype(F32)
        for i in range(4):
            t32[i] = wide[:, i * 128:i * 128 + 128]
        for p in range(4):
            for i in range(4):
                dst[pl.ds(h * 512 + p * F, F), i * 128:i * 128 + 128] = (
                    t32[i, pl.ds(p, F, stride=4), :].astype(BF))

    def forward_dense(h):
        base = h * 512
        rows = pl.ds(base, 512)
        by_pixel(rl, x_s, h)
        xx = x_s[rows, :]
        frame = row_of((512, C)) % F
        conv = jnp.where(frame == 0, 0.0, pltpu.roll(nn(xx, wc[0]), 1, 0))
        conv = conv + nn(xx, wc[1])
        conv = conv + jnp.where(frame == F - 1, 0.0, pltpu.roll(nn(xx, wc[2]), 511, 0))
        mid = (xx.astype(F32) + conv).astype(BF)
        mid_s[rows, :] = mid
        upper = mid.astype(F32)
        rinv = lax.rsqrt(jnp.mean(upper * upper, -1, keepdims=True) + 1e-06)
        normed = (upper * rinv * gain[...]).astype(BF)
        nt_s[h] = normed.T
        xt_s[h] = xx.T
        for i, weight in enumerate((wq, wk, wv)):
            qkv_s[rows, i * C:(i + 1) * C] = nn(normed, weight[...]).astype(BF)

    def forward_attend(p):
        rows = pl.ds(pl.multiple_of(p * F, F), F)
        cols = pl.ds(pl.multiple_of(p % 4 * F, F), F)
        scores = []
        for j in range(4):
            q = qkv_s[rows, j * 128:j * 128 + 128]
            k2 = split_heads(qkv_s[rows, C + j * 128:C + j * 128 + 128])
            scores.append((nt(k2, q) * 0.125).reshape(2, F, F))
        for j in range(4):
            e = jnp.exp(scores[j] - jnp.max(scores[j], 1, keepdims=True))
            probs = (e * (1.0 / jnp.sum(e, 1, keepdims=True))).reshape(2 * F, F)
            pr_s[p * 4 + j] = probs
            v2 = split_heads(qkv_s[rows, 2 * C + j * 128:2 * C + j * 128 + 128])
            at_s[p // 4, j * 128:j * 128 + 128, cols] = tn(v2, probs.astype(BF)).astype(BF)

    for h in range(2):
        arrived(rl, h, h)
        if h == 0:
            scatter(sbu, ru, 0, 2)
        forward_dense(h)
        if h == 1:
            scatter(sbu, ru, 1, 3)

        @pl.loop(4 * h, 4 * h + 4)
        def _(p):
            forward_attend(p)

    def backward_att(h):
        base = h * 512
        rows = pl.ds(base, 512)
        by_pixel(ru, up_s, h)
        da_s[rows, :] = nt(up_s[rows, :], wo[...]).astype(BF)

    def backward_valued(p):
        rows = pl.ds(pl.multiple_of(p * F, F), F)
        for j in range(4):
            da = da_s[rows, j * 128:j * 128 + 128]
            dv = join_heads(nn(pr_s[p * 4 + j].astype(BF), da)).astype(BF)
            dqkv_s[rows, 2 * C + j * 128:2 * C + j * 128 + 128] = dv

    def backward_attend(p):
        rows = pl.ds(pl.multiple_of(p * F, F), F)
        lanes = [slice(j * 128, j * 128 + 128) for j in range(4)]
        da = [da_s[rows, ln] for ln in lanes]
        probs = [pr_s[p * 4 + j] for j in range(4)]
        dp = [
            nt(split_heads(qkv_s[rows, 2 * C + j * 128:2 * C + j * 128 + 128]), da[j])
            for j in range(4)
        ]
        ds = []
        for j in range(4):
            p3, d3 = probs[j].reshape(2, F, F), dp[j].reshape(2, F, F)
            d = p3 * (d3 - jnp.sum(p3 * d3, 1, keepdims=True)) * 0.125
            ds.append(d.reshape(2 * F, F).astype(BF))
        for j in range(4):
            q = qkv_s[rows, lanes[j]]
            dk = join_heads(nn(ds[j], q)).astype(BF)
            dqkv_s[rows, C + j * 128:C + j * 128 + 128] = dk
        for j in range(4):
            k2 = split_heads(qkv_s[rows, C + j * 128:C + j * 128 + 128])
            dqkv_s[rows, lanes[j]] = tn(ds[j], k2).astype(BF)

    def put(i, h, value):
        value = value.reshape(16, 2, 16, C)
        if h == 0:
            g_s[i] = value
        else:
            g_s[i] = g_s[i] + value

    def grad_outer(h):
        put(6, h, nn(at_s[h], up_s[pl.ds(h * 512, 512), :]))

    def grad_weight(i, h):
        put(3 + i, h, nn(nt_s[h], dqkv_s[pl.ds(h * 512, 512), i * C:(i + 1) * C]))

    def grad_tap(i, h):
        put(i, h, nn(xt_s[h], dm_s[pl.ds(h * 512, 512), i * C:(i + 1) * C]))

    def backward_norm(h):
        base = h * 512
        rows = pl.ds(base, 512)
        d_normed = nt(dqkv_s[rows, 0:C], wq[...])
        d_normed = d_normed + nt(dqkv_s[rows, C:2 * C], wk[...])
        d_normed = d_normed + nt(dqkv_s[rows, 2 * C:3 * C], wv[...])
        upper = mid_s[rows, :].astype(F32)
        rinv = lax.rsqrt(jnp.mean(upper * upper, -1, keepdims=True) + 1e-06)
        term = jnp.sum(d_normed * upper * rinv, 0, keepdims=True)
        if h == 0:
            gain_s[...] = term
        else:
            gain_s[...] = gain_s[...] + term
        scaled = gain[...] * d_normed
        mean = jnp.mean(scaled * upper, -1, keepdims=True)
        d_mid = up_s[rows, :].astype(F32) + rinv * scaled - upper * (rinv * rinv * rinv) * mean
        d_mid = d_mid.astype(BF)
        wide = d_mid.astype(F32)
        frame = row_of((512, C)) % F
        dm_s[rows, 0:C] = jnp.where(frame == F - 1, 0.0, pltpu.roll(wide, 511, 0)).astype(BF)
        dm_s[rows, C:2 * C] = d_mid
        dm_s[rows, 2 * C:3 * C] = jnp.where(frame == 0, 0.0, pltpu.roll(wide, 1, 0)).astype(BF)

    def backward_conv(h):
        rows = pl.ds(h * 512, 512)
        back = nt(dm_s[rows, 0:C], wc[0])
        back = back + nt(dm_s[rows, C:2 * C], wc[1])
        back = back + nt(dm_s[rows, 2 * C:3 * C], wc[2])
        grad = dm_s[rows, C:2 * C].astype(F32) + back
        for p in range(4):
            for i in range(4):
                t32[i, pl.ds(p, F, stride=4), :] = (
                    grad[p * F:(p + 1) * F, i * 128:i * 128 + 128])
        for i in range(4):
            osend[h, :, :, i * 128:i * 128 + 128] = t32[i].astype(BF).reshape(TM, 16, 128)

    sib = device(zl, 1 - c, x, y, zh)
    owner = c == zh
    not_owner = jnp.logical_not(owner)

    def to_x(to):
        return device(zl, c, to, y, zh)

    def to_y(to):
        return device(zl, c, x, to, zh)

    def red_cores(g):
        r = red[g]
        for i, m in enumerate(GROUPS[g]):
            r["g0s"][:, i] = g_s[m, :, 1 - c].astype(BF)
        send(r["g0s"], r["g0r"], ssem.at[6 + 7 * g], rsem.at[6 + 7 * g], sib)

    def red_first(g):
        r, s = red[g], 7 + 7 * g
        wait_bytes(r["g0r"], rsem.at[6 + 7 * g])
        for i, m in enumerate(GROUPS[g]):
            for xx in range(4):
                four = slice(xx * 4, xx * 4 + 4)
                both = g_s[m, four, c] + r["g0r"][four, i].astype(F32)
                r["s1x"][xx, :, i] = both[:, :, :256].astype(BF)
                r["s1y"][:, xx, i] = both[:, :, 256:].astype(BF)

        @pl.loop(1, 4)
        def _(k):
            tx, ty = (x + k) % 4, (y + k) % 4
            send(r["s1x"].at[tx], r["r1x"].at[x], ssem.at[s], rsem.at[s], to_x(tx))
            send(r["s1y"].at[ty], r["r1y"].at[y], ssem.at[s + 1], rsem.at[s + 1], to_y(ty))

    def total(ref, own, mine):
        acc = own[mine].astype(F32)
        for k in range(1, 4):
            acc = acc + ref[(mine + k) % 4].astype(F32)
        return acc

    def red_second(g):
        r, s = red[g], 7 + 7 * g
        wait_bytes(r["r1x"].at[pl.ds(0, 3)], rsem.at[s])
        r["s2x"][...] = total(r["r1x"], r["s1x"], x).astype(BF)

        @pl.loop(1, 4)
        def _(k):
            ty = (y + k) % 4
            send(r["s2x"].at[ty], r["r2x"].at[y], ssem.at[s + 2], rsem.at[s + 2], to_y(ty))

        wait_bytes(r["r1y"].at[pl.ds(0, 3)], rsem.at[s + 1])
        r["s2y"][...] = total(r["r1y"], r["s1y"], y).astype(BF)

        @pl.loop(1, 4)
        def _(k):
            tx = (x + k) % 4
            send(r["s2y"].at[tx], r["r2y"].at[x], ssem.at[s + 3], rsem.at[s + 3], to_x(tx))

    def red_z(g):
        r, s = red[g], 7 + 7 * g
        wait_bytes(r["r2x"].at[pl.ds(0, 3)], rsem.at[s + 2])
        half = total(r["r2x"], r["s2x"], y).astype(BF)
        r["ts"][0] = half[:, :, :128]
        r["ts"][1] = half[:, :, 128:]
        wait_bytes(r["r2y"].at[pl.ds(0, 3)], rsem.at[s + 3])
        half = total(r["r2y"], r["s2y"], x).astype(BF)
        r["ts"][2] = half[:, :, :128]
        r["ts"][3] = half[:, :, 128:]

        @pl.loop(0, 4)
        def _(k):
            q = (zl + k) % 4

            @pl.when(jnp.logical_or(not_owner, k != 0))
            def _():
                send(r["ts"].at[q], r["zr"].at[z], ssem.at[s + 4], rsem.at[s + 4],
                     at_z(c * 4 + q, c))

    def red_gather(g):
        r, s = red[g], 7 + 7 * g

        @pl.when(owner)
        def _():
            r["zr"][z] = r["ts"][zl]
            wait_bytes(r["zr"].at[pl.ds(0, 7)], rsem.at[s + 4])
            acc = r["zr"][0].astype(F32)
            for k in range(1, 8):
                acc = acc + r["zr"][k].astype(F32)
            agr[g][zl] = acc.astype(BF)

            @pl.loop(1, 8)
            def _(k):
                to = (zl * 2 + c + k) % 8
                send(agr[g].at[zl], agr[g].at[zl], ssem.at[s + 5], rsem.at[s + 5],
                     at_z(zh * 4 + to // 2, to % 2))

    def red_end(g):
        r, s = red[g], 7 + 7 * g

        @pl.when(owner)
        def _():
            wait_bytes(agr[g].at[pl.ds(0, 3)], rsem.at[s + 5])
            wait_bytes(r["ts"].at[pl.ds(0, 3)], ssem.at[s + 4])
            wait_bytes(r["zr"].at[pl.ds(0, 7)], ssem.at[s + 5])

        @pl.when(not_owner)
        def _():
            wait_bytes(agr[g], rsem.at[s + 5])
            wait_bytes(r["ts"], ssem.at[s + 4])

        wait_bytes(r["g0s"], ssem.at[6 + 7 * g])
        wait_bytes(r["s1x"].at[pl.ds(0, 3)], ssem.at[s])
        wait_bytes(r["s1y"].at[pl.ds(0, 3)], ssem.at[s + 1])
        wait_bytes(r["s2x"].at[pl.ds(0, 3)], ssem.at[s + 2])
        wait_bytes(r["s2y"].at[pl.ds(0, 3)], ssem.at[s + 3])

    def gain_cores():
        gn_s[...] = jnp.concatenate(
            [gain_s[:, i * 128:(i + 1) * 128] for i in range(4)] + [jnp.zeros((4, 128), F32)], 0)
        send(gn_s, gn0, ssem.at[GS], rsem.at[GS], sib)

    def gain_x():
        wait_bytes(gn0, rsem.at[GS])
        gnx[x] = gn_s[...] + gn0[...]

        @pl.loop(1, 4)
        def _(k):
            send(gnx.at[x], gnx.at[x], ssem.at[GS + 1], rsem.at[GS + 1], to_x((x + k) % 4))

    def gain_y():
        wait_bytes(gnx.at[pl.ds(0, 3)], rsem.at[GS + 1])
        gny[y] = gnx[0] + gnx[1] + gnx[2] + gnx[3]

        @pl.loop(1, 4)
        def _(k):
            send(gny.at[y], gny.at[y], ssem.at[GS + 2], rsem.at[GS + 2], to_y((y + k) % 4))

    def gain_z():
        wait_bytes(gny.at[pl.ds(0, 3)], rsem.at[GS + 2])
        gnz[z] = gny[0] + gny[1] + gny[2] + gny[3]

        @pl.loop(1, 8)
        def _(k):
            send(gnz.at[z], gnz.at[z], ssem.at[GS + 3], rsem.at[GS + 3], at_z((z + k) % 8, c))

    def gain_end():
        wait_bytes(gnz.at[pl.ds(0, 7)], rsem.at[GS + 3])
        acc = gnz[0]
        for k in range(1, 8):
            acc = acc + gnz[k]
        ogain[...] = acc
        wait_bytes(gn_s, ssem.at[GS])
        wait_bytes(gnx.at[pl.ds(0, 3)], ssem.at[GS + 1])
        wait_bytes(gny.at[pl.ds(0, 3)], ssem.at[GS + 2])
        wait_bytes(gnz.at[pl.ds(0, 7)], ssem.at[GS + 3])

    own_out = [pltpu.make_async_copy(osend.at[h, me], orecv.at[h, me], lsem.at[7 + h])
               for h in range(2)]

    arrived(ru, 0, 2)
    backward_att(0)

    @pl.loop(0, 4)
    def _(p):
        backward_valued(p)
        backward_attend(p)

    grad_outer(0)
    for i in range(3):
        grad_weight(i, 0)
    backward_norm(0)
    for i in range(3):
        grad_tap(i, 0)
    backward_conv(0)
    scatter(osend, orecv, 0, 4)
    own_out[0].start()

    arrived(ru, 1, 3)
    backward_att(1)

    @pl.loop(4, 8)
    def _(p):
        backward_valued(p)

    grad_outer(1)
    grad_weight(2, 1)
    red_cores(0)

    @pl.loop(4, 6)
    def _(p):
        backward_attend(p)

    red_first(0)

    @pl.loop(6, 8)
    def _(p):
        backward_attend(p)

    grad_weight(0, 1)
    grad_weight(1, 1)
    red_cores(1)
    backward_norm(1)
    red_first(1)
    grad_tap(0, 1)
    red_cores(2)
    grad_tap(1, 1)
    red_cores(3)
    gain_cores()
    red_first(2)
    grad_tap(2, 1)
    red_cores(4)
    red_first(3)
    backward_conv(1)
    red_first(4)
    scatter(osend, orecv, 1, 5)
    own_out[1].start()
    red_second(0)
    gain_x()
    red_second(1)
    red_second(2)
    red_z(0)
    gain_y()
    red_second(3)
    red_z(1)
    red_second(4)
    red_z(2)
    gain_z()
    red_z(3)
    red_z(4)
    for g in range(NG):
        red_gather(g)
    for g in range(NG):
        red_end(g)
    gain_end()

    for h in range(2):
        arrived(orecv, h, 4 + h)
        own_out[h].wait()
    for i, ref in enumerate((sbl, sbl, sbu, sbu, osend, osend)):
        wait_bytes(ref.at[i % 2, pl.ds(0, TM - 1)], ssem.at[i])


def finish(orecv, og0, og1, og2, og3, og4, ogain, out, conv, query, key, value, outer, gain):
    low = row_of((F, C)) % 8 < 4
    for h in range(2):
        got = [[], [], [], []]
        for m in range(16):
            for o in range(2):
                tile = orecv[h, 2 * m + o].astype(F32)
                got[o].append(tile[0:8])
                got[2 + o].append(tile[8:16])
        got = [jnp.concatenate(g, 0) for g in got]
        for f in (0, 2):
            even, odd = got[f], got[f + 1]
            out[f, 128 * h:128 * h + 128, :] = jnp.where(
                low, even, pltpu.roll(odd, 4, 0)).astype(BF)
            out[f + 1, 128 * h:128 * h + 128, :] = jnp.where(
                low, pltpu.roll(even, F - 4, 0), odd).astype(BF)
    for q in range(4):
        lanes = slice(q * 128, q * 128 + 128)
        outer[:, lanes] = og0[q, 0].astype(F32)
        value[:, lanes] = og0[q, 1].astype(F32)
        query[:, lanes] = og1[q, 0].astype(F32)
        key[:, lanes] = og1[q, 1].astype(F32)
        for i, ref in enumerate((og2, og3, og4)):
            conv[i, :, lanes] = ref[q, 0].astype(F32)
    tm = lax.axis_index("tm")
    row = ogain[pl.ds(tm // 8, 1), :]
    gain[...] = pltpu.roll(row, (128 - (tm % 8) * 16) % 128, 1)[0, :16]


def block(latents, upstream, conv_weight, w_query, w_key, w_value, w_out, norm_gain):
    v = lambda shape, dtype=BF: pltpu.VMEM(shape, dtype)
    scratch = [
        v((4, 256, C)), v((4, 256, C)), v((3, C, C)), v((C, C)), v((C, C)), v((C, C)), v((C, C)),
        v((2, TM, 16, C)), v((2, TM, 16, C)), v((2, TM, 16, C)), v((2, TM, 16, C)),
        v((2, TM, 16, C)),
        v((4, 512, 128), F32), v((1024, C)), v((1024, C)),
        v((2, C, 512)), v((2, C, 512)), v((2, C, 512)), v((1024, 3 * C)),
        v((32, 256, F), F32), v((1024, C)), v((1024, C)),
        v((1024, 3 * C)), v((1024, 3 * C)),
        v((7, 16, 2, 16, C), F32), v((1, C), F32),
        v((8, 128), F32), v((8, 128), F32), v((4, 8, 128), F32), v((4, 8, 128), F32),
        v((8, 8, 128), F32),
    ]
    for group in GROUPS:
        n = len(group)
        scratch += [v((16, n, 16, C))] * 2 + [v((4, 4, n, 16, 256))] * 4
        scratch += [v((4, n, 16, 256))] * 4 + [v((4, n, 16, 128)), v((8, n, 16, 128))]
    scratch += [pltpu.SemaphoreType.DMA((GS + 4,)), pltpu.SemaphoreType.DMA((GS + 4,)),
                pltpu.SemaphoreType.DMA((9,))]
    vmem = pl.BlockSpec(memory_space=pltpu.VMEM)
    hbm = pl.BlockSpec(memory_space=pl.ANY)
    got = pl.pallas_call(
        kernel,
        out_shape=(
            jax.ShapeDtypeStruct((2, TM, 16, C), BF),
            *[jax.ShapeDtypeStruct((4, len(g), 16, 128), BF) for g in GROUPS],
            jax.ShapeDtypeStruct((8, 128), F32),
        ),
        in_specs=[hbm] * 7 + [vmem],
        out_specs=(hbm, *[vmem] * (NG + 1)),
        scratch_shapes=scratch,
        compiler_params=pltpu.CompilerParams(
            collective_id=0, has_side_effects=True, vmem_limit_bytes=60 * 2**20
        ),
        name="block_backward",
    )(latents, upstream, conv_weight, w_query, w_key, w_value, w_out, norm_gain)
    rows = jax.ShapeDtypeStruct((16, C), F32)
    return pl.pallas_call(
        finish,
        out_shape=(
            jax.ShapeDtypeStruct((4, 256, C), BF),
            jax.ShapeDtypeStruct((3, 16, C), F32),
            rows, rows, rows, rows,
            jax.ShapeDtypeStruct((16,), F32),
        ),
        in_specs=[vmem] * (NG + 2),
        out_specs=(vmem,) * 7,
        name="finish",
    )(*got)


def per_device(latents, upstream, conv_weight, w_query, w_key, w_value, w_out, norm_gain):
    grad_in, *grads = block(
        latents[0], upstream[0], conv_weight, w_query, w_key, w_value, w_out, norm_gain[None]
    )
    return (grad_in[None], *grads)


def solution(mesh):
    return jax.shard_map(
        per_device,
        mesh=mesh,
        in_specs=(P("dp", "tm", None, None), P("dp", "tm", None, None),
                  P(), P(), P(), P(), P(), P()),
        out_specs=(
            P("dp", "tm", None, None),
            P(None, "tm", None),
            P("tm", None),
            P("tm", None),
            P("tm", None),
            P("tm", None),
            P("tm"),
        ),
        check_vma=False,
    )
```

```python
import jax
import jax.numpy as jnp
from jax import lax
from jax.experimental import pallas as pl
from jax.experimental.pallas import tpu as pltpu
from jax.sharding import PartitionSpec as P

C = 512
F = 128
TM = 32
BF = jnp.bfloat16
F32 = jnp.float32
MESH_ID = pl.DeviceIdType.MESH


def nn(a, b):
    return lax.dot_general(a, b, (((1,), (0,)), ((), ())), preferred_element_type=F32)


def nt(a, b):
    return lax.dot_general(a, b, (((1,), (1,)), ((), ())), preferred_element_type=F32)


def tn(a, b):
    return lax.dot_general(a, b, (((0,), (0,)), ((), ())), preferred_element_type=F32)


def where_am_i():
    dp, tm = lax.axis_index("dp"), lax.axis_index("tm")
    return dict(dp=dp, tm=tm, zl=dp // 2, c=dp % 2, x=tm // 8, y=(tm // 2) % 4, zh=tm % 2)


def device(zl, c, x, y, zh):
    return {"dp": zl * 2 + c, "tm": (x * 4 + y) * 2 + zh}


def signal(sem, dev):
    pl.semaphore_signal(sem, inc=1, device_id=dev, device_id_type=MESH_ID)


def send(src, dst, ssem, rsem, dev):
    pltpu.make_async_remote_copy(
        src_ref=src, dst_ref=dst, send_sem=ssem, recv_sem=rsem,
        device_id=dev, device_id_type=MESH_ID,
    ).start()


def wait_bytes(ref, sem):
    pltpu.make_async_copy(ref, ref, sem).wait()


def row_of(shape):
    return lax.broadcasted_iota(jnp.int32, shape, 0)


def split_heads(a):
    lane = lax.broadcasted_iota(jnp.int32, a.shape, 1)
    zero = jnp.zeros_like(a)
    return jnp.concatenate([jnp.where(lane < 64, a, zero), jnp.where(lane < 64, zero, a)], 0)


def join_heads(a):
    lane = lax.broadcasted_iota(jnp.int32, (F, 128), 1)
    return jnp.where(lane < 64, a[:F], a[F:])


GROUPS = ((6, 5), (3, 4), (0,), (1,), (2,))
NG = len(GROUPS)
GS = 6 + 7 * NG


def kernel(
    lat_in, up_in, wc_in, wq_in, wk_in, wv_in, wo_in, gain,
    orecv, og0, og1, og2, og3, og4, ogain,
    lat, up, wc, wq, wk, wv, wo,
    sbl, sbu, rl, ru, osend,
    t32, x_s, mid_s, nt_s, xt_s, at_s, qkv_s, pr_s, up_s, da_s, dqkv_s, dm_s,
    g_s, gain_s, gn_s, gn0, gnx, gny, gnz,
    *rest,
):
    ssem, rsem, lsem = rest[-3:]
    red = [dict(zip(("g0s", "g0r", "s1x", "r1x", "s1y", "r1y", "s2x", "r2x", "s2y", "r2y",
                     "ts", "zr"), rest[12 * i:12 * i + 12])) for i in range(NG)]
    agr = (og0, og1, og2, og3, og4)
    loads = [
        pltpu.make_async_copy(src, dst, lsem.at[i])
        for i, (src, dst) in enumerate(
            ((lat_in, lat), (up_in, up), (wc_in, wc), (wq_in, wq), (wk_in, wk),
             (wv_in, wv), (wo_in, wo)))
    ]
    for load in loads:
        load.start()
    w = where_am_i()
    me, c, x, y, zl, zh = w["tm"], w["c"], w["x"], w["y"], w["zl"], w["zh"]
    z = zh * 4 + zl

    def at_z(zz, cc):
        return device(zz % 4, cc, x, y, zz // 4)

    barrier = pltpu.get_barrier_semaphore()

    @pl.loop(1, TM)
    def _(k):
        signal(barrier, {"dp": w["dp"], "tm": (me + k) % TM})

    signal(barrier, device(zl, 1 - c, x, y, zh))

    @pl.loop(1, 8)
    def _(k):
        @pl.when(k != 4)
        def _():
            signal(barrier, at_z((z + k) % 8, c))

    @pl.loop(1, 4)
    def _(k):
        signal(barrier, at_z(zh * 4 + (zl + k) % 4, 1 - c))

    def regroup(src, dst, h):
        a = [src[f, 128 * h:128 * h + 128, :].astype(F32) for f in range(4)]
        low = row_of((F, C)) % 8 < 4
        tiles = []
        for f in (0, 2):
            even = jnp.where(low, a[f], pltpu.roll(a[f + 1], 4, 0))
            odd = jnp.where(low, pltpu.roll(a[f], F - 4, 0), a[f + 1])
            tiles.append((even.reshape(16, 8, C), odd.reshape(16, 8, C)))
        for m in range(16):
            for o in range(2):
                dst[h, 2 * m + o] = jnp.concatenate(
                    [tiles[0][o][m], tiles[1][o][m]], 0
                ).astype(BF)

    def scatter(src, dst, h, i, lo=1, step=1):
        @pl.loop(lo, TM, step=step)
        def _(k):
            to = (me + k) % TM
            send(src.at[h, to], dst.at[h, me], ssem.at[i], rsem.at[i],
                 {"dp": w["dp"], "tm": to})

    def arrived(dst, h, i):
        wait_bytes(dst.at[h, pl.ds(0, TM - 1)], rsem.at[i])

    loads[0].wait()
    regroup(lat, sbl, 0)
    regroup(lat, sbl, 1)
    pl.semaphore_wait(barrier, 41)
    scatter(sbl, rl, 0, 0)
    scatter(sbl, rl, 1, 1)
    for h in range(2):
        rl[h, me] = sbl[h, me]
    loads[1].wait()
    regroup(up, sbu, 0)
    regroup(up, sbu, 1)
    for h in range(2):
        ru[h, me] = sbu[h, me]
    for load in loads[2:]:
        load.wait()

    def by_pixel(src, dst, h):
        wide = src[h].reshape(512, C).astype(F32)
        for i in range(4):
            t32[i] = wide[:, i * 128:i * 128 + 128]
        for p in range(4):
            for i in range(4):
                dst[pl.ds(h * 512 + p * F, F), i * 128:i * 128 + 128] = (
                    t32[i, pl.ds(p, F, stride=4), :].astype(BF))

    def forward_dense(h):
        base = h * 512
        rows = pl.ds(base, 512)
        by_pixel(rl, x_s, h)
        xx = x_s[rows, :]
        frame = row_of((512, C)) % F
        conv = jnp.where(frame == 0, 0.0, pltpu.roll(nn(xx, wc[0]), 1, 0))
        conv = conv + nn(xx, wc[1])
        conv = conv + jnp.where(frame == F - 1, 0.0, pltpu.roll(nn(xx, wc[2]), 511, 0))
        mid = (xx.astype(F32) + conv).astype(BF)
        mid_s[rows, :] = mid
        upper = mid.astype(F32)
        rinv = lax.rsqrt(jnp.mean(upper * upper, -1, keepdims=True) + 1e-06)
        normed = (upper * rinv * gain[...]).astype(BF)
        nt_s[h] = normed.T
        xt_s[h] = xx.T
        for i, weight in enumerate((wq, wk, wv)):
            qkv_s[rows, i * C:(i + 1) * C] = nn(normed, weight[...]).astype(BF)

    def forward_attend(p):
        rows = pl.ds(pl.multiple_of(p * F, F), F)
        cols = pl.ds(pl.multiple_of(p % 4 * F, F), F)
        scores = []
        for j in range(4):
            q = qkv_s[rows, j * 128:j * 128 + 128]
            k2 = split_heads(qkv_s[rows, C + j * 128:C + j * 128 + 128])
            scores.append((nt(k2, q) * 0.125).reshape(2, F, F))
        for j in range(4):
            e = jnp.exp(scores[j] - jnp.max(scores[j], 1, keepdims=True))
            probs = (e * (1.0 / jnp.sum(e, 1, keepdims=True))).reshape(2 * F, F)
            pr_s[p * 4 + j] = probs
            v2 = split_heads(qkv_s[rows, 2 * C + j * 128:2 * C + j * 128 + 128])
            at_s[p // 4, j * 128:j * 128 + 128, cols] = tn(v2, probs.astype(BF)).astype(BF)

    for h in range(2):
        arrived(rl, h, h)
        if h == 0:
            scatter(sbu, ru, 0, 2)
        forward_dense(h)
        if h == 1:
            scatter(sbu, ru, 1, 3)

        @pl.loop(4 * h, 4 * h + 4)
        def _(p):
            forward_attend(p)

    def backward_att(h):
        base = h * 512
        rows = pl.ds(base, 512)
        by_pixel(ru, up_s, h)
        da_s[rows, :] = nt(up_s[rows, :], wo[...]).astype(BF)

    def backward_valued(p):
        rows = pl.ds(pl.multiple_of(p * F, F), F)
        for j in range(4):
            da = da_s[rows, j * 128:j * 128 + 128]
            dv = join_heads(nn(pr_s[p * 4 + j].astype(BF), da)).astype(BF)
            dqkv_s[rows, 2 * C + j * 128:2 * C + j * 128 + 128] = dv

    def backward_attend(p):
        rows = pl.ds(pl.multiple_of(p * F, F), F)
        lanes = [slice(j * 128, j * 128 + 128) for j in range(4)]
        da = [da_s[rows, ln] for ln in lanes]
        probs = [pr_s[p * 4 + j] for j in range(4)]
        dp = [
            nt(split_heads(qkv_s[rows, 2 * C + j * 128:2 * C + j * 128 + 128]), da[j])
            for j in range(4)
        ]
        ds = []
        for j in range(4):
            p3, d3 = probs[j].reshape(2, F, F), dp[j].reshape(2, F, F)
            d = p3 * (d3 - jnp.sum(p3 * d3, 1, keepdims=True)) * 0.125
            ds.append(d.reshape(2 * F, F).astype(BF))
        for j in range(4):
            q = qkv_s[rows, lanes[j]]
            dk = join_heads(nn(ds[j], q)).astype(BF)
            dqkv_s[rows, C + j * 128:C + j * 128 + 128] = dk
        for j in range(4):
            k2 = split_heads(qkv_s[rows, C + j * 128:C + j * 128 + 128])
            dqkv_s[rows, lanes[j]] = tn(ds[j], k2).astype(BF)

    def put(i, h, value):
        value = value.reshape(16, 2, 16, C)
        if h == 0:
            g_s[i] = value
        else:
            g_s[i] = g_s[i] + value

    def grad_outer(h):
        put(6, h, nn(at_s[h], up_s[pl.ds(h * 512, 512), :]))

    def grad_weight(i, h):
        put(3 + i, h, nn(nt_s[h], dqkv_s[pl.ds(h * 512, 512), i * C:(i + 1) * C]))

    def grad_tap(i, h):
        put(i, h, nn(xt_s[h], dm_s[pl.ds(h * 512, 512), i * C:(i + 1) * C]))

    def backward_norm(h):
        base = h * 512
        rows = pl.ds(base, 512)
        d_normed = nt(dqkv_s[rows, 0:C], wq[...])
        d_normed = d_normed + nt(dqkv_s[rows, C:2 * C], wk[...])
        d_normed = d_normed + nt(dqkv_s[rows, 2 * C:3 * C], wv[...])
        upper = mid_s[rows, :].astype(F32)
        rinv = lax.rsqrt(jnp.mean(upper * upper, -1, keepdims=True) + 1e-06)
        term = jnp.sum(d_normed * upper * rinv, 0, keepdims=True)
        if h == 0:
            gain_s[...] = term
        else:
            gain_s[...] = gain_s[...] + term
        scaled = gain[...] * d_normed
        mean = jnp.mean(scaled * upper, -1, keepdims=True)
        d_mid = up_s[rows, :].astype(F32) + rinv * scaled - upper * (rinv * rinv * rinv) * mean
        d_mid = d_mid.astype(BF)
        wide = d_mid.astype(F32)
        frame = row_of((512, C)) % F
        dm_s[rows, 0:C] = jnp.where(frame == F - 1, 0.0, pltpu.roll(wide, 511, 0)).astype(BF)
        dm_s[rows, C:2 * C] = d_mid
        dm_s[rows, 2 * C:3 * C] = jnp.where(frame == 0, 0.0, pltpu.roll(wide, 1, 0)).astype(BF)

    def backward_conv(h):
        rows = pl.ds(h * 512, 512)
        back = nt(dm_s[rows, 0:C], wc[0])
        back = back + nt(dm_s[rows, C:2 * C], wc[1])
        back = back + nt(dm_s[rows, 2 * C:3 * C], wc[2])
        grad = dm_s[rows, C:2 * C].astype(F32) + back
        for p in range(4):
            for i in range(4):
                t32[i, pl.ds(p, F, stride=4), :] = (
                    grad[p * F:(p + 1) * F, i * 128:i * 128 + 128])
        for i in range(4):
            osend[h, :, :, i * 128:i * 128 + 128] = t32[i].astype(BF).reshape(TM, 16, 128)

    sib = device(zl, 1 - c, x, y, zh)
    owner = c == zh
    not_owner = jnp.logical_not(owner)

    def to_x(to):
        return device(zl, c, to, y, zh)

    def to_y(to):
        return device(zl, c, x, to, zh)

    def red_cores(g):
        r = red[g]
        for i, m in enumerate(GROUPS[g]):
            r["g0s"][:, i] = g_s[m, :, 1 - c].astype(BF)
        send(r["g0s"], r["g0r"], ssem.at[6 + 7 * g], rsem.at[6 + 7 * g], sib)

    def red_first(g):
        r, s = red[g], 7 + 7 * g
        wait_bytes(r["g0r"], rsem.at[6 + 7 * g])
        for i, m in enumerate(GROUPS[g]):
            for xx in range(4):
                four = slice(xx * 4, xx * 4 + 4)
                both = g_s[m, four, c] + r["g0r"][four, i].astype(F32)
                r["s1x"][xx, :, i] = both[:, :, :256].astype(BF)
                r["s1y"][:, xx, i] = both[:, :, 256:].astype(BF)

        @pl.loop(1, 4)
        def _(k):
            tx, ty = (x + k) % 4, (y + k) % 4
            send(r["s1x"].at[tx], r["r1x"].at[x], ssem.at[s], rsem.at[s], to_x(tx))
            send(r["s1y"].at[ty], r["r1y"].at[y], ssem.at[s + 1], rsem.at[s + 1], to_y(ty))

    def total(ref, own, mine):
        acc = own[mine].astype(F32)
        for k in range(1, 4):
            acc = acc + ref[(mine + k) % 4].astype(F32)
        return acc

    def red_second(g):
        r, s = red[g], 7 + 7 * g
        wait_bytes(r["r1x"].at[pl.ds(0, 3)], rsem.at[s])
        r["s2x"][...] = total(r["r1x"], r["s1x"], x).astype(BF)

        @pl.loop(1, 4)
        def _(k):
            ty = (y + k) % 4
            send(r["s2x"].at[ty], r["r2x"].at[y], ssem.at[s + 2], rsem.at[s + 2], to_y(ty))

        wait_bytes(r["r1y"].at[pl.ds(0, 3)], rsem.at[s + 1])
        r["s2y"][...] = total(r["r1y"], r["s1y"], y).astype(BF)

        @pl.loop(1, 4)
        def _(k):
            tx = (x + k) % 4
            send(r["s2y"].at[tx], r["r2y"].at[x], ssem.at[s + 3], rsem.at[s + 3], to_x(tx))

    def red_z(g):
        r, s = red[g], 7 + 7 * g
        wait_bytes(r["r2x"].at[pl.ds(0, 3)], rsem.at[s + 2])
        half = total(r["r2x"], r["s2x"], y).astype(BF)
        r["ts"][0] = half[:, :, :128]
        r["ts"][1] = half[:, :, 128:]
        wait_bytes(r["r2y"].at[pl.ds(0, 3)], rsem.at[s + 3])
        half = total(r["r2y"], r["s2y"], x).astype(BF)
        r["ts"][2] = half[:, :, :128]
        r["ts"][3] = half[:, :, 128:]

        @pl.loop(0, 4)
        def _(k):
            q = (zl + k) % 4

            @pl.when(jnp.logical_or(not_owner, k != 0))
            def _():
                send(r["ts"].at[q], r["zr"].at[z], ssem.at[s + 4], rsem.at[s + 4],
                     at_z(c * 4 + q, c))

    def red_gather(g):
        r, s = red[g], 7 + 7 * g

        @pl.when(owner)
        def _():
            r["zr"][z] = r["ts"][zl]
            wait_bytes(r["zr"].at[pl.ds(0, 7)], rsem.at[s + 4])
            acc = r["zr"][0].astype(F32)
            for k in range(1, 8):
                acc = acc + r["zr"][k].astype(F32)
            agr[g][zl] = acc.astype(BF)

            @pl.loop(1, 8)
            def _(k):
                to = (zl * 2 + c + k) % 8
                send(agr[g].at[zl], agr[g].at[zl], ssem.at[s + 5], rsem.at[s + 5],
                     at_z(zh * 4 + to // 2, to % 2))

    def red_end(g):
        r, s = red[g], 7 + 7 * g

        @pl.when(owner)
        def _():
            wait_bytes(agr[g].at[pl.ds(0, 3)], rsem.at[s + 5])
            wait_bytes(r["ts"].at[pl.ds(0, 3)], ssem.at[s + 4])
            wait_bytes(r["zr"].at[pl.ds(0, 7)], ssem.at[s + 5])

        @pl.when(not_owner)
        def _():
            wait_bytes(agr[g], rsem.at[s + 5])
            wait_bytes(r["ts"], ssem.at[s + 4])

        wait_bytes(r["g0s"], ssem.at[6 + 7 * g])
        wait_bytes(r["s1x"].at[pl.ds(0, 3)], ssem.at[s])
        wait_bytes(r["s1y"].at[pl.ds(0, 3)], ssem.at[s + 1])
        wait_bytes(r["s2x"].at[pl.ds(0, 3)], ssem.at[s + 2])
        wait_bytes(r["s2y"].at[pl.ds(0, 3)], ssem.at[s + 3])

    def gain_cores():
        gn_s[...] = jnp.concatenate(
            [gain_s[:, i * 128:(i + 1) * 128] for i in range(4)] + [jnp.zeros((4, 128), F32)], 0)
        send(gn_s, gn0, ssem.at[GS], rsem.at[GS], sib)

    def gain_x():
        wait_bytes(gn0, rsem.at[GS])
        gnx[x] = gn_s[...] + gn0[...]

        @pl.loop(1, 4)
        def _(k):
            send(gnx.at[x], gnx.at[x], ssem.at[GS + 1], rsem.at[GS + 1], to_x((x + k) % 4))

    def gain_y():
        wait_bytes(gnx.at[pl.ds(0, 3)], rsem.at[GS + 1])
        gny[y] = gnx[0] + gnx[1] + gnx[2] + gnx[3]

        @pl.loop(1, 4)
        def _(k):
            send(gny.at[y], gny.at[y], ssem.at[GS + 2], rsem.at[GS + 2], to_y((y + k) % 4))

    def gain_z():
        wait_bytes(gny.at[pl.ds(0, 3)], rsem.at[GS + 2])
        gnz[z] = gny[0] + gny[1] + gny[2] + gny[3]

        @pl.loop(1, 8)
        def _(k):
            send(gnz.at[z], gnz.at[z], ssem.at[GS + 3], rsem.at[GS + 3], at_z((z + k) % 8, c))

    def gain_end():
        wait_bytes(gnz.at[pl.ds(0, 7)], rsem.at[GS + 3])
        acc = gnz[0]
        for k in range(1, 8):
            acc = acc + gnz[k]
        ogain[...] = acc
        wait_bytes(gn_s, ssem.at[GS])
        wait_bytes(gnx.at[pl.ds(0, 3)], ssem.at[GS + 1])
        wait_bytes(gny.at[pl.ds(0, 3)], ssem.at[GS + 2])
        wait_bytes(gnz.at[pl.ds(0, 7)], ssem.at[GS + 3])

    own_out = [pltpu.make_async_copy(osend.at[h, me], orecv.at[h, me], lsem.at[7 + h])
               for h in range(2)]

    arrived(ru, 0, 2)
    backward_att(0)

    @pl.loop(0, 4)
    def _(p):
        backward_valued(p)
        backward_attend(p)

    grad_outer(0)
    for i in range(3):
        grad_weight(i, 0)
    backward_norm(0)
    for i in range(3):
        grad_tap(i, 0)
    backward_conv(0)
    scatter(osend, orecv, 0, 4)
    own_out[0].start()

    arrived(ru, 1, 3)
    backward_att(1)

    @pl.loop(4, 8)
    def _(p):
        backward_valued(p)

    grad_outer(1)
    grad_weight(2, 1)
    red_cores(0)

    @pl.loop(4, 6)
    def _(p):
        backward_attend(p)

    red_first(0)

    @pl.loop(6, 8)
    def _(p):
        backward_attend(p)

    grad_weight(0, 1)
    grad_weight(1, 1)
    red_cores(1)
    backward_norm(1)
    red_first(1)
    grad_tap(0, 1)
    red_cores(2)
    grad_tap(1, 1)
    red_cores(3)
    gain_cores()
    red_first(2)
    grad_tap(2, 1)
    red_cores(4)
    red_first(3)
    backward_conv(1)
    red_first(4)
    scatter(osend, orecv, 1, 5, 1, 2)
    red_second(0)
    gain_x()
    red_second(1)
    red_second(2)
    red_z(0)
    gain_y()
    red_second(3)
    red_z(1)
    red_second(4)
    red_z(2)
    gain_z()
    red_z(3)
    red_z(4)
    scatter(osend, orecv, 1, 5, 2, 2)
    own_out[1].start()
    for g in range(NG):
        red_gather(g)
    for g in range(NG):
        red_end(g)
    gain_end()

    for h in range(2):
        arrived(orecv, h, 4 + h)
        own_out[h].wait()
    for i, ref in enumerate((sbl, sbl, sbu, sbu, osend, osend)):
        wait_bytes(ref.at[i % 2, pl.ds(0, TM - 1)], ssem.at[i])


def finish(orecv, og0, og1, og2, og3, og4, ogain, out, conv, query, key, value, outer, gain):
    low = row_of((F, C)) % 8 < 4
    for h in range(2):
        got = [[], [], [], []]
        for m in range(16):
            for o in range(2):
                tile = orecv[h, 2 * m + o].astype(F32)
                got[o].append(tile[0:8])
                got[2 + o].append(tile[8:16])
        got = [jnp.concatenate(g, 0) for g in got]
        for f in (0, 2):
            even, odd = got[f], got[f + 1]
            out[f, 128 * h:128 * h + 128, :] = jnp.where(
                low, even, pltpu.roll(odd, 4, 0)).astype(BF)
            out[f + 1, 128 * h:128 * h + 128, :] = jnp.where(
                low, pltpu.roll(even, F - 4, 0), odd).astype(BF)
    for q in range(4):
        lanes = slice(q * 128, q * 128 + 128)
        outer[:, lanes] = og0[q, 0].astype(F32)
        value[:, lanes] = og0[q, 1].astype(F32)
        query[:, lanes] = og1[q, 0].astype(F32)
        key[:, lanes] = og1[q, 1].astype(F32)
        for i, ref in enumerate((og2, og3, og4)):
            conv[i, :, lanes] = ref[q, 0].astype(F32)
    tm = lax.axis_index("tm")
    row = ogain[pl.ds(tm // 8, 1), :]
    gain[...] = pltpu.roll(row, (128 - (tm % 8) * 16) % 128, 1)[0, :16]


def block(latents, upstream, conv_weight, w_query, w_key, w_value, w_out, norm_gain):
    v = lambda shape, dtype=BF: pltpu.VMEM(shape, dtype)
    scratch = [
        v((4, 256, C)), v((4, 256, C)), v((3, C, C)), v((C, C)), v((C, C)), v((C, C)), v((C, C)),
        v((2, TM, 16, C)), v((2, TM, 16, C)), v((2, TM, 16, C)), v((2, TM, 16, C)),
        v((2, TM, 16, C)),
        v((4, 512, 128), F32), v((1024, C)), v((1024, C)),
        v((2, C, 512)), v((2, C, 512)), v((2, C, 512)), v((1024, 3 * C)),
        v((32, 256, F), F32), v((1024, C)), v((1024, C)),
        v((1024, 3 * C)), v((1024, 3 * C)),
        v((7, 16, 2, 16, C), F32), v((1, C), F32),
        v((8, 128), F32), v((8, 128), F32), v((4, 8, 128), F32), v((4, 8, 128), F32),
        v((8, 8, 128), F32),
    ]
    for group in GROUPS:
        n = len(group)
        scratch += [v((16, n, 16, C))] * 2 + [v((4, 4, n, 16, 256))] * 4
        scratch += [v((4, n, 16, 256))] * 4 + [v((4, n, 16, 128)), v((8, n, 16, 128))]
    scratch += [pltpu.SemaphoreType.DMA((GS + 4,)), pltpu.SemaphoreType.DMA((GS + 4,)),
                pltpu.SemaphoreType.DMA((9,))]
    vmem = pl.BlockSpec(memory_space=pltpu.VMEM)
    hbm = pl.BlockSpec(memory_space=pl.ANY)
    got = pl.pallas_call(
        kernel,
        out_shape=(
            jax.ShapeDtypeStruct((2, TM, 16, C), BF),
            *[jax.ShapeDtypeStruct((4, len(g), 16, 128), BF) for g in GROUPS],
            jax.ShapeDtypeStruct((8, 128), F32),
        ),
        in_specs=[hbm] * 7 + [vmem],
        out_specs=(hbm, *[vmem] * (NG + 1)),
        scratch_shapes=scratch,
        compiler_params=pltpu.CompilerParams(
            collective_id=0, has_side_effects=True, vmem_limit_bytes=60 * 2**20
        ),
        name="block_backward",
    )(latents, upstream, conv_weight, w_query, w_key, w_value, w_out, norm_gain)
    rows = jax.ShapeDtypeStruct((16, C), F32)
    return pl.pallas_call(
        finish,
        out_shape=(
            jax.ShapeDtypeStruct((4, 256, C), BF),
            jax.ShapeDtypeStruct((3, 16, C), F32),
            rows, rows, rows, rows,
            jax.ShapeDtypeStruct((16,), F32),
        ),
        in_specs=[vmem] * (NG + 2),
        out_specs=(vmem,) * 7,
        name="finish",
    )(*got)


def per_device(latents, upstream, conv_weight, w_query, w_key, w_value, w_out, norm_gain):
    grad_in, *grads = block(
        latents[0], upstream[0], conv_weight, w_query, w_key, w_value, w_out, norm_gain[None]
    )
    return (grad_in[None], *grads)


def solution(mesh):
    return jax.shard_map(
        per_device,
        mesh=mesh,
        in_specs=(P("dp", "tm", None, None), P("dp", "tm", None, None),
                  P(), P(), P(), P(), P(), P()),
        out_specs=(
            P("dp", "tm", None, None),
            P(None, "tm", None),
            P("tm", None),
            P("tm", None),
            P("tm", None),
            P("tm", None),
            P("tm"),
        ),
        check_vma=False,
    )
```
